512 devices in a mesh: role: 2 (over core), inst: 16 (over z_lo, y), tp: 16 (over z_hi, x).
Axes of the slice: x: 4, y: 4, z: 16 (z_hi: 4, z_lo: 4; z = z_hi * 4 + z_lo), core: 2. Of those that a mesh axis runs over, the one named last changes fastest.
Arguments:
- hidden: bfloat16 [2, 16, 256, 8192], P('role', 'inst', None, 'tp'), may hold values from -6 to 6
- queries: bfloat16 [2, 16, 256, 16384], P('role', 'inst', None, 'tp'), may hold values from -120 to 120
- prefix_cache: bfloat16 [2, 16, 16, 2, 2048, 128], P('role', 'inst', 'tp'), may hold values from -4 to 4
- lengths: int32 [2, 16], P('role', 'inst'), may hold values from 1 to 32, as said below
- pairing: int32 [16], replicated, may hold values from 0 to 15, as said below
- w_kv: bfloat16 [8192, 2048], P('tp'), may hold values from -0.0625 to 0.0625
Outputs:
- attended: bfloat16 [2, 16, 256, 16384], P('role', 'inst', None, 'tp')
- layer_kv: bfloat16 [2, 16, 256, 2048], P('role', 'inst', None, 'tp')
The draws below stay inside these ranges and needn't reach their ends.
Inputs may be any that keep to these rules, and one draw needn't show every extreme that they name: `lengths`: every request has at least one cached block; some request holds all 32 blocks. `pairing`: each decode instance takes over exactly one prefill instance; for some decode instance j, it is prefill instance (j + 8) mod 16.
All inputs are finite; a program needn't handle non-finite values.
Results may differ from the reference program's by a relative error of at most 0.0052.
Values may be sent and summed in bfloat16 or wider, within the bound.
No kernel may reach another device: no remote copies, remote signals or barrier semaphores. Data moves between devices by JAX's collectives and lax.ppermute only.
A program may use at most 64 MiB of HBM per device.

```python
import math
import jax
import jax.numpy as jnp
from jax import lax

D = 8192
HEAD_DIM = 128
HEADS_DEV = 8
BLOCK = 128
NEWTOK = 256
PREFIX = 4096
KV_HEADS = 8
QDIM = 16384
KVDIM = 2048
PREFIX_BLOCKS = 32
INSTANCES = 16


def cache_base(key):
    return jnp.clip(jax.random.normal(key, (2, INSTANCES, 2 * KV_HEADS, 2, PREFIX // 2, HEAD_DIM), jnp.float32), -4.0, 4.0)


def draw_prefix_cache(key, part):
    cache_vals = cache_base(key)
    return cache_vals.astype(jnp.bfloat16)


def draw_queries(key, part):
    key = jax.random.fold_in(key, 7)
    query_vals = jnp.clip(jax.random.normal(key, (2, INSTANCES, NEWTOK, QDIM), jnp.float32), -4.0, 4.0)
    return query_vals.astype(jnp.bfloat16)


def draw_lengths(key, part):
    key = jax.random.fold_in(key, 5)
    first_key, second_key = jax.random.split(key)
    drawn = jax.random.randint(first_key, (2 * INSTANCES,), 1, PREFIX_BLOCKS + 1)
    chosen = jax.random.randint(second_key, (), 0, 2 * INSTANCES)
    filled = jnp.where(jnp.arange(2 * INSTANCES) == chosen, PREFIX_BLOCKS, drawn)
    return filled.reshape(2, INSTANCES).astype(jnp.int32)


def draw_pairing(key, part):
    key = jax.random.fold_in(key, 11)
    perm_key, pick_key = jax.random.split(key)
    shuffled = jax.random.permutation(perm_key, jnp.arange(INSTANCES, dtype=jnp.int32)).astype(jnp.int32)
    target = jax.random.randint(pick_key, (), 0, INSTANCES).astype(jnp.int32)
    sender = ((target + INSTANCES // 2) % INSTANCES).astype(jnp.int32)
    holder = jnp.sum(jnp.where(shuffled == target, jnp.arange(INSTANCES, dtype=jnp.int32), 0)).astype(jnp.int32)
    displaced = shuffled[sender]
    shuffled = shuffled.at[holder].set(displaced)
    shuffled = shuffled.at[sender].set(target)
    return shuffled.astype(jnp.int32)


def level_of(rng, extent, cuts, least, largest):
    def one(axis_at, blocks):
        steps = jax.random.uniform(jax.random.fold_in(jax.random.fold_in(rng, 6), axis_at), (blocks,), jnp.float32, least / len(cuts), largest / len(cuts))
        return jnp.repeat(jnp.exp(steps), extent[axis_at] // blocks).reshape((-1,) + (1,) * (len(extent) - axis_at - 1))

    level = one(*cuts[0])
    for cut in cuts[1:]:
        level = level * one(*cut)
    return level


def gaussian(own_key, shape, scale, reach, shards=(), held_as=jnp.bfloat16):
    array = jax.random.normal(own_key, shape, jnp.float32) * scale
    if len(shards) > 0:
        array = level_of(own_key, shape, shards, -0.22, 0.18) * array
    return jnp.clip(array, min=-reach, max=reach).astype(held_as)


def setup_inputs(seed: int = 0) -> dict:
    keys = jax.random.split(jax.random.key(seed), 7)
    hidden = gaussian(keys[0], (2, INSTANCES, NEWTOK, D), 1.0, 6.0, ((0, 2), (1, 16), (3, 16)))
    queries = draw_queries(jax.random.fold_in(keys[6], 71), 0)
    prefix_cache = draw_prefix_cache(jax.random.fold_in(keys[6], 71), 0)
    lengths = draw_lengths(jax.random.fold_in(keys[6], 71), 0)
    pairing = draw_pairing(jax.random.fold_in(keys[6], 71), 0)
    w_kv = gaussian(keys[5], (D, KVDIM), D ** -0.5, 0.0625, ((0, 16),))
    return dict(hidden=hidden, queries=queries, prefix_cache=prefix_cache, lengths=lengths, pairing=pairing, w_kv=w_kv)


def rotate(key_rows, positions):
    half_dim = key_rows.shape[-1] // 2
    steps_range = jnp.arange(half_dim).astype(jnp.float32)
    frequency = jnp.exp(steps_range * (-2.0 * math.log(500000.0) / key_rows.shape[-1]))
    angles = positions[:, None] * frequency[None, :]
    angles = angles.reshape((angles.shape[0],) + (1,) * (key_rows.ndim - 2) + (half_dim,))
    cosine = jnp.cos(angles)
    sine_term = jnp.sin(angles)
    front_half = key_rows[..., :half_dim]
    back_half = key_rows[..., half_dim:]
    return jnp.concatenate([front_half * cosine - back_half * sine_term, back_half * cosine + front_half * sine_term], axis=-1)


def attend(queried, keys_all, values_all, limit_rows, new_len):
    prefix_len = keys_all.shape[0] - new_len
    scores = lax.dot_general(queried, keys_all, (((1,), (1,)), ((), ())), preferred_element_type=jnp.float32)
    scores = scores * (queried.shape[-1] ** -0.5)
    key_pos = jnp.arange(keys_all.shape[0])[None, :]
    row_pos = (jnp.arange(queried.shape[0]) % new_len)[:, None]
    allowed = (key_pos < limit_rows) | ((key_pos >= prefix_len) & (key_pos - prefix_len <= row_pos))
    masked = jnp.where(allowed, scores, -jnp.inf)
    row_max = jnp.max(masked, axis=1, keepdims=True)
    weights = jnp.exp(masked - row_max)
    weight_sum = jnp.sum(weights, axis=1, keepdims=True)
    product = jnp.dot(weights.astype(jnp.bfloat16), values_all, preferred_element_type=jnp.float32)
    return (product / weight_sum).astype(jnp.bfloat16)


def reference(hidden, queries, prefix_cache, lengths, pairing, w_kv):
    request_count = 2 * INSTANCES
    token_all = hidden.reshape(request_count, NEWTOK, D)
    queries_all = queries.reshape(request_count, NEWTOK, QDIM)
    caches_all = prefix_cache.reshape(request_count, KV_HEADS, 2, 2, PREFIX // 2, HEAD_DIM)
    lengths_all = lengths.reshape(request_count)
    group_width = 2 * HEADS_DEV * HEAD_DIM

    def one_request(packed):
        token_rows, query_rows, cache_rows, length = packed
        summed = jnp.dot(token_rows, w_kv, preferred_element_type=jnp.float32).reshape(NEWTOK, KV_HEADS, 2, HEAD_DIM)
        positions = (length * BLOCK + jnp.arange(NEWTOK)).astype(jnp.float32)
        rotated = rotate(summed[:, :, 0], positions)
        fresh_kv = jnp.stack([rotated, summed[:, :, 1]], axis=2).astype(jnp.bfloat16)
        ordered = cache_rows.transpose(0, 2, 1, 3, 4).reshape(KV_HEADS, 2, PREFIX, HEAD_DIM)

        def one_group(group_id):
            keys_all = jnp.concatenate([ordered[group_id, 0], fresh_kv[:, group_id, 0]], axis=0)
            values_all = jnp.concatenate([ordered[group_id, 1], fresh_kv[:, group_id, 1]], axis=0)
            picked = lax.dynamic_slice_in_dim(query_rows, group_id * group_width, group_width, 1)
            stacked = picked.reshape(NEWTOK, 2 * HEADS_DEV, HEAD_DIM).transpose(1, 0, 2).reshape(-1, HEAD_DIM)
            result = attend(stacked, keys_all, values_all, length * BLOCK, NEWTOK)
            return result.reshape(2 * HEADS_DEV, NEWTOK, HEAD_DIM).transpose(1, 0, 2).reshape(NEWTOK, group_width)

        grouped = lax.map(one_group, jnp.arange(KV_HEADS).astype(jnp.int32))
        attended_rows = grouped.transpose(1, 0, 2).reshape(NEWTOK, QDIM)
        return attended_rows, fresh_kv.reshape(NEWTOK, KVDIM)

    attended, fresh_all = lax.map(one_request, (token_all, queries_all, caches_all, lengths_all))
    attended = attended.reshape(2, INSTANCES, NEWTOK, QDIM)
    fresh_all = fresh_all.reshape(2, INSTANCES, NEWTOK, KVDIM)
    handed = jnp.zeros((INSTANCES, NEWTOK, KVDIM), jnp.bfloat16).at[pairing].set(fresh_all[0])
    layer_kv = jnp.stack([fresh_all[0], handed], axis=0)
    return attended, layer_kv
```

```python
import functools
import math

import jax
import jax.numpy as jnp
from jax import lax
from jax.experimental import pallas as pl
from jax.experimental.pallas import tpu as pltpu
from jax.sharding import PartitionSpec as P

BLOCK = 128
HD = 128
TOK = 256
HALF = 2048
HEADS = 8
STEP_HEADS = 2
CHUNKS = 2
CHUNK = HALF // CHUNKS
LOW = -1e30
SCALE = HD**-0.5 * math.log2(math.e)
VMEM_LIMIT = 40 * 1024 * 1024


def swap_tp(array, mask):
    return lax.ppermute(array, "tp", [(i, i ^ mask) for i in range(16)])


def role_inst(array, pairs):
    return lax.ppermute(array, ("role", "inst"), pairs)


def project_kernel(at_ref, hidden_ref, w_ref, own_ref, *send_refs):
    x, zh = at_ref[0], at_ref[1]
    for j in (1, 2, 3, 0):
        for k in range(4):
            column = pl.multiple_of(((zh ^ k) * 4 + (x ^ j)) * HD, HD)
            part = jnp.dot(
                hidden_ref[...], w_ref[:, pl.ds(column, HD)], preferred_element_type=jnp.float32
            )
            if j == 0:
                own_ref[k] = part
            else:
                send_refs[j - 1][k] = part.astype(jnp.bfloat16)


def project(hidden, w_kv, x, zh):
    vmem = pl.BlockSpec(memory_space=pltpu.VMEM)
    return pl.pallas_call(
        project_kernel,
        out_shape=[jax.ShapeDtypeStruct((4, TOK, HD), jnp.float32)]
        + [jax.ShapeDtypeStruct((4, TOK, HD), jnp.bfloat16)] * 3,
        in_specs=[pl.BlockSpec(memory_space=pltpu.SMEM), vmem, vmem],
        out_specs=[vmem] * 4,
        compiler_params=pltpu.CompilerParams(vmem_limit_bytes=VMEM_LIMIT),
        cost_estimate=pl.CostEstimate(
            flops=2 * TOK * 512 * 2048, bytes_accessed=4 << 20, transcendentals=0
        ),
        name="project",
    )(jnp.stack([x, zh]), hidden, w_kv)


def dot_rows(a, b):
    return lax.dot_general(a, b, (((1,), (1,)), ((), ())), preferred_element_type=jnp.float32)


def attend_kernel(first, last, *refs):
    refs = list(refs)
    valid_ref, q_ref, kv_ref = refs[:3]
    refs = refs[3:]
    if not first:
        acc_in, stat_in = refs[:2]
        refs = refs[2:]
    if last:
        fresh_k, fresh_v = refs[:2]
        refs = refs[2:]
        out_ref = refs[0]
        refs = refs[1:]
    else:
        acc_out, stat_out = refs[:2]
        refs = refs[2:]
    keys, values = refs[:2]
    if last:
        fresh_ext = refs[2]
    step = pl.program_id(0)
    valid = valid_ref[0]
    count = keys.shape[0]

    @pl.when(step == 0)
    def prepare():
        inside = lax.broadcasted_iota(jnp.int32, (count, HD), 0) < valid
        rows = kv_ref[0]
        keys[...] = jnp.where(inside, rows, jnp.broadcast_to(rows[:1], rows.shape))
        values[:, :HD] = jnp.where(inside, kv_ref[1], 0)
        values[:, HD:] = jnp.where(inside, 1.0, 0.0).astype(jnp.bfloat16)
        if last:
            fresh_ext[:, :HD] = fresh_v[...]
            fresh_ext[:, HD:] = jnp.ones((TOK, HD), jnp.bfloat16)

    lane = lax.broadcasted_iota(jnp.int32, (TOK, HD), 1)

    def state(at):
        if first:
            return (
                jnp.full((TOK, 1), LOW, jnp.float32),
                jnp.zeros((TOK, HD), jnp.float32),
                jnp.zeros((TOK, HD), jnp.float32),
            )
        head = step * STEP_HEADS + at
        stats = stat_in[...]
        top = jnp.sum(jnp.where(lane == head, stats, 0.0), axis=1, keepdims=True)
        total = jnp.sum(jnp.where(lane == head + HEADS, stats, 0.0), axis=1, keepdims=True)
        acc = acc_in[:, at * HD : (at + 1) * HD]
        return top, jnp.broadcast_to(total, (TOK, HD)), acc

    def store(at, top, total, acc):
        if last:
            out_ref[:, at * HD : (at + 1) * HD] = (acc / total).astype(jnp.bfloat16)
        else:
            head = step * STEP_HEADS + at
            acc_out[:, at * HD : (at + 1) * HD] = acc
            stat_out[...] = jnp.where(
                lane == head,
                jnp.broadcast_to(top, (TOK, HD)),
                jnp.where(lane == head + HEADS, total, stat_out[...]),
            )

    def compute(with_cache):
        for at in range(STEP_HEADS):
            queried = q_ref[:, at * HD : (at + 1) * HD]
            top, total, acc = state(at)
            scores = []
            if with_cache:
                scores.append(dot_rows(queried, keys[...]))
            if last:
                new = dot_rows(queried, fresh_k[...])
                row = lax.broadcasted_iota(jnp.int32, (TOK, TOK), 0)
                column = lax.broadcasted_iota(jnp.int32, (TOK, TOK), 1)
                scores.append(jnp.where(column <= row, new, LOW))
            peak = top
            for block in scores:
                peak = jnp.maximum(peak, jnp.max(block, axis=1, keepdims=True))
            shift = peak * SCALE
            ext = None
            for index, block in enumerate(scores):
                weights = jnp.exp2(block * SCALE - shift).astype(jnp.bfloat16)
                holder = values if with_cache and index == 0 else fresh_ext
                term = jnp.dot(weights, holder[...], preferred_element_type=jnp.float32)
                ext = term if ext is None else ext + term
            if ext is None:
                store(at, top, total, acc)
            elif first:
                store(at, peak, ext[:, HD:], ext[:, :HD])
            else:
                decay = jnp.exp2((top - peak) * SCALE)
                store(at, peak, total * decay + ext[:, HD:], acc * decay + ext[:, :HD])

    if not last:

        @pl.when(step == 0)
        def clear():
            stat_out[...] = jnp.zeros_like(stat_out)

    pl.when(valid > 0)(lambda: compute(True))
    pl.when(valid <= 0)(lambda: compute(False))


def attend(valid, queries, cache, chunk, count, state=None, fresh=None):
    first, last = state is None, fresh is not None
    wide = STEP_HEADS * HD
    heads_spec = pl.BlockSpec((TOK, wide), lambda h: (0, h))
    whole = pl.BlockSpec((TOK, HD), lambda h: (0, 0))
    in_specs = [
        pl.BlockSpec(memory_space=pltpu.SMEM),
        heads_spec,
        pl.BlockSpec((2, count, HD), lambda h: (0, chunk, 0)),
    ]
    args = [valid.reshape(1), queries, cache]
    if not first:
        in_specs += [heads_spec, whole]
        args += list(state)
    scratch = [pltpu.VMEM((count, HD), jnp.bfloat16), pltpu.VMEM((count, 2 * HD), jnp.bfloat16)]
    if last:
        in_specs += [whole, whole]
        args += list(fresh)
        scratch.append(pltpu.VMEM((TOK, 2 * HD), jnp.bfloat16))
        out_shape = jax.ShapeDtypeStruct((TOK, HEADS * HD), jnp.bfloat16)
        out_specs = heads_spec
    else:
        out_shape = [
            jax.ShapeDtypeStruct((TOK, HEADS * HD), jnp.float32),
            jax.ShapeDtypeStruct((TOK, HD), jnp.float32),
        ]
        out_specs = [heads_spec, whole]
    slots = count + (TOK if last else 0)
    return pl.pallas_call(
        functools.partial(attend_kernel, first, last),
        grid=(HEADS // STEP_HEADS,),
        out_shape=out_shape,
        in_specs=in_specs,
        out_specs=out_specs,
        scratch_shapes=scratch,
        compiler_params=pltpu.CompilerParams(vmem_limit_bytes=VMEM_LIMIT),
        cost_estimate=pl.CostEstimate(
            flops=8 * TOK * HEADS * slots * HD,
            bytes_accessed=4 << 20,
            transcendentals=TOK * HEADS * slots,
        ),
        name="attend_last" if last else ("attend_first" if first else "attend_more"),
    )(*args)


def rotation(positions, is_key):
    half = HD // 2
    frequency = jnp.exp(jnp.arange(half).astype(jnp.float32) * (-2.0 * math.log(500000.0) / HD))
    angles = positions[:, None] * frequency[None, :]
    cosine = jnp.where(is_key, jnp.cos(angles), 1.0)
    sine = jnp.where(is_key, jnp.sin(angles), 0.0)
    return cosine, sine


def per_device(hidden, queries, prefix_cache, lengths, pairing, w_kv):
    member = lax.axis_index("tp")
    inst = lax.axis_index("inst")
    role = lax.axis_index("role")
    x, zh = member % 4, member // 4
    y, zl = inst % 4, inst // 4
    is_key = member % 2 == 0
    length = lengths[0, 0]
    limit = length * BLOCK
    low_valid = jnp.minimum(limit, HALF)
    high_valid = limit - low_valid
    own_valid = jnp.where(is_key, low_valid, high_valid)
    other_valid = jnp.where(is_key, high_valid, low_valid)
    resident = prefix_cache[0, 0, 0]
    queried = queries[0, 0]

    own, *sends = project(hidden[0, 0], w_kv, x, zh)
    with jax.named_scope("sum_x"):
        arrived = [swap_tp(sends[j - 1], j) for j in (1, 2, 3)]
    with jax.named_scope("prefix"):
        across = [
            swap_tp(resident[:, c * CHUNK : (c + 1) * CHUNK], 1) for c in range(CHUNKS)
        ]
    summed = own
    for block in arrived:
        summed = summed + block.astype(jnp.float32)
    with jax.named_scope("sum_z"):
        arrived = [swap_tp(summed[k].astype(jnp.bfloat16), 4 * k) for k in (1, 2, 3)]
    total = summed[0]
    for block in arrived:
        total = total + block.astype(jnp.float32)
    cosine, sine = rotation((limit + jnp.arange(TOK)).astype(jnp.float32), is_key)
    front, back = total[:, : HD // 2], total[:, HD // 2 :]
    own_kv = jnp.concatenate(
        [front * cosine - back * sine, back * cosine + front * sine], axis=1
    ).astype(jnp.bfloat16)

    with jax.named_scope("pair"):
        other_kv = swap_tp(own_kv, 1)
    keys_new = jnp.where(is_key, own_kv, other_kv)
    values_new = jnp.where(is_key, other_kv, own_kv)

    with jax.named_scope("attention"):
        state = attend(own_valid, queried, resident, 0, HALF)
        for c in range(CHUNKS - 1):
            valid = jnp.clip(other_valid - c * CHUNK, 0, CHUNK)
            state = attend(valid, queried, across[c], 0, CHUNK, state)
        valid = jnp.clip(other_valid - (CHUNKS - 1) * CHUNK, 0, CHUNK)
        attended = attend(
            valid, queried, across[-1], 0, CHUNK, state, (keys_new, values_new)
        )

    slots = jnp.arange(16, dtype=jnp.int32)
    sources = jnp.sum(jnp.where(pairing[None, :] == slots[:, None], slots[None, :], 0), axis=1)
    with jax.named_scope("handoff_y"):
        column = [own_kv] + [
            role_inst(own_kv, [(i, i ^ j) for i in range(16)]) for j in (1, 2, 3)
        ]
    column = jnp.stack(column)
    with jax.named_scope("handoff_z"):
        offers = []
        for j in range(4):
            source = sources[(zl ^ j) * 4 + y]
            offer = lax.dynamic_index_in_dim(column, (source % 4) ^ y, 0, keepdims=False)
            offers.append(role_inst(offer, [(i, 16 + (i ^ (4 * j))) for i in range(16)]))
    handed = lax.dynamic_index_in_dim(
        jnp.stack(offers), (sources[inst] // 4) ^ zl, 0, keepdims=False
    )
    layer_kv = jnp.where(role == 1, handed, own_kv)
    return attended[None, None], layer_kv[None, None]


def solution(mesh):
    in_specs = (
        P("role", "inst", None, "tp"),
        P("role", "inst", None, "tp"),
        P("role", "inst", "tp", None, None, None),
        P("role", "inst"),
        P(),
        P("tp", None),
    )
    out_specs = (P("role", "inst", None, "tp"), P("role", "inst", None, "tp"))
    return jax.shard_map(
        per_device, mesh=mesh, in_specs=in_specs, out_specs=out_specs, check_vma=False
    )
```

```python
import functools
import math

import jax
import jax.numpy as jnp
from jax import lax
from jax.experimental import pallas as pl
from jax.experimental.pallas import tpu as pltpu
from jax.sharding import PartitionSpec as P

BLOCK = 128
HD = 128
TOK = 256
HALF = 2048
HEADS = 8
STEP_HEADS = 4
SUB = 512
FEATURES = 512
LOW = -1e30
SCALE = HD**-0.5 * math.log2(math.e)

SMEM = pl.BlockSpec(memory_space=pltpu.SMEM)
VMEM = pl.BlockSpec(memory_space=pltpu.VMEM)
HBM = pl.BlockSpec(memory_space=pltpu.HBM)
ANY = pl.BlockSpec(memory_space=pl.ANY)


def params(mib):
    return pltpu.CompilerParams(vmem_limit_bytes=mib * 1024 * 1024)


def struct(shape, dtype):
    return jax.ShapeDtypeStruct(shape, dtype)


def swap_tp(array, mask):
    return lax.ppermute(array, "tp", [(i, i ^ mask) for i in range(16)])


def role_inst(array, pairs):
    return lax.ppermute(array, ("role", "inst"), pairs)


def project_kernel(member_ref, hidden_hbm, w_hbm, own_ref, *rest):
    send_refs, (hidden, weights, hidden_sem, sems) = rest[:3], rest[3:]
    member = member_ref[0]
    order = [(j, k) for j in (2, 3, 1, 0) for k in range(4)]
    fetch_hidden = pltpu.make_async_copy(hidden_hbm, hidden, hidden_sem)
    fetch_hidden.start()
    copies = []
    for slot, (j, k) in enumerate(order):
        column = pl.multiple_of((member ^ (4 * k + j)) * HD, HD)
        copy = pltpu.make_async_copy(
            w_hbm.at[:, pl.ds(column, HD)], weights.at[slot], sems.at[slot]
        )
        copy.start()
        copies.append(copy)
    fetch_hidden.wait()
    for slot, (j, k) in enumerate(order):
        copies[slot].wait()
        part = jnp.dot(hidden[...], weights[slot], preferred_element_type=jnp.float32)
        if j == 0:
            own_ref[k] = part
        else:
            send_refs[j - 1][k] = part.astype(jnp.bfloat16)


def project(member, hidden, w_kv):
    return pl.pallas_call(
        project_kernel,
        out_shape=[struct((4, TOK, HD), jnp.float32)] + [struct((4, TOK, HD), jnp.bfloat16)] * 3,
        in_specs=[SMEM, HBM, HBM],
        out_specs=[VMEM] * 4,
        scratch_shapes=[
            pltpu.VMEM((TOK, FEATURES), jnp.bfloat16),
            pltpu.VMEM((16, FEATURES, HD), jnp.bfloat16),
            pltpu.SemaphoreType.DMA,
            pltpu.SemaphoreType.DMA((16,)),
        ],
        compiler_params=params(60),
        cost_estimate=pl.CostEstimate(
            flops=2 * TOK * FEATURES * 2048, bytes_accessed=4 << 20, transcendentals=0
        ),
        name="project",
    )(member, hidden, w_kv)


def sum_x_kernel(own_ref, a_ref, b_ref, c_ref, after_ref, keep_ref, *send_refs):
    for k in range(4):
        total = own_ref[k] + a_ref[k].astype(jnp.float32)
        total = total + b_ref[k].astype(jnp.float32) + c_ref[k].astype(jnp.float32)
        if k == 0:
            keep_ref[...] = total
        else:
            send_refs[k - 1][...] = total.astype(jnp.bfloat16)


def sum_x(own, arrived, after):
    return pl.pallas_call(
        sum_x_kernel,
        out_shape=[struct((TOK, HD), jnp.float32)] + [struct((TOK, HD), jnp.bfloat16)] * 3,
        in_specs=[VMEM] * 4 + [ANY],
        out_specs=[VMEM] * 4,
        compiler_params=params(8),
        name="sum_x",
    )(own, *arrived, after)


def finish_kernel(keep_ref, a_ref, b_ref, c_ref, cosine_ref, sine_ref, after_ref, out_ref):
    total = keep_ref[...] + a_ref[...].astype(jnp.float32)
    total = total + b_ref[...].astype(jnp.float32) + c_ref[...].astype(jnp.float32)
    turned = pltpu.roll(total, HD // 2, 1)
    out_ref[...] = (total * cosine_ref[...] + turned * sine_ref[...]).astype(jnp.bfloat16)


def finish(keep, arrived, cosine, sine, after):
    return pl.pallas_call(
        finish_kernel,
        out_shape=struct((TOK, HD), jnp.bfloat16),
        in_specs=[VMEM] * 6 + [ANY],
        out_specs=VMEM,
        compiler_params=params(8),
        name="finish",
    )(keep, *arrived, cosine, sine, after)


def source_of(pairing_ref, target):
    source = jnp.int32(0)
    for i in range(16):
        source = jnp.where(pairing_ref[i] == target, i, source)
    return source


def choose(index, refs):
    block = refs[0][...]
    for at in range(1, len(refs)):
        block = jnp.where(index == at, refs[at][...], block)
    return block


def offer_kernel(pairing_ref, inst_ref, *refs):
    column, outs = refs[:4], refs[4:]
    inst = inst_ref[0]
    for j in range(4):
        source = source_of(pairing_ref, inst ^ (4 * j))
        outs[j][...] = choose((source ^ inst) & 3, column)


def offer(pairing, inst, column):
    return pl.pallas_call(
        offer_kernel,
        out_shape=[struct((TOK, HD), jnp.bfloat16)] * 4,
        in_specs=[SMEM] * 2 + [VMEM] * 4,
        out_specs=[VMEM] * 4,
        compiler_params=params(8),
        name="offer",
    )(pairing, inst, *column)


def take_kernel(pairing_ref, inst_ref, role_ref, own_ref, *refs):
    offers, out_ref = refs[:4], refs[5]
    inst = inst_ref[0]
    source = source_of(pairing_ref, inst)
    handed = choose((source ^ inst) // 4, offers)
    out_ref[...] = jnp.where(role_ref[0] == 1, handed, own_ref[...])


def take(pairing, inst, role, own_kv, offers, after):
    return pl.pallas_call(
        take_kernel,
        out_shape=struct((TOK, HD), jnp.bfloat16),
        in_specs=[SMEM] * 3 + [VMEM] * 5 + [ANY],
        out_specs=VMEM,
        compiler_params=params(8),
        name="take",
    )(pairing, inst, role, own_kv, *offers, after)


def dot_rows(a, b):
    return lax.dot_general(a, b, (((1,), (1,)), ((), ())), preferred_element_type=jnp.float32)


def load_cache(valid, kv_ref, keys, values):
    inside = lax.broadcasted_iota(jnp.int32, (HALF, HD), 0) < valid
    rows = kv_ref[0]
    keys[...] = jnp.where(inside, rows, jnp.broadcast_to(rows[:1], rows.shape))
    values[:, :HD] = jnp.where(inside, kv_ref[1], 0)
    values[:, HD:] = jnp.where(inside, 1.0, 0.0).astype(jnp.bfloat16)


def update(top, ext, scores, values):
    peak = jnp.max(scores, axis=1, keepdims=True) * SCALE
    if top is not None:
        peak = jnp.maximum(top, peak)
    weights = jnp.exp2(scores * SCALE - peak).astype(jnp.bfloat16)
    term = jnp.dot(weights, values, preferred_element_type=jnp.float32)
    if top is not None:
        term = ext * jnp.exp2(top - peak) + term
    return peak, term


def over_cache(top, ext, queried, keys, values):
    for at in range(0, HALF, SUB):
        scores = dot_rows(queried, keys[at : at + SUB, :])
        top, ext = update(top, ext, scores, values[at : at + SUB, :])
    return top, ext


def own_half_kernel(aliased, length_ref, member_ref, q_ref, kv_ref, *refs):
    refs = refs[3:] if aliased else refs[1:]
    acc_ref, stat_ref, keys, values = refs
    limit = length_ref[0] * BLOCK
    low = jnp.minimum(limit, HALF)
    valid = jnp.where(member_ref[0] % 2 == 0, low, limit - low)
    lane = lax.broadcasted_iota(jnp.int32, (TOK, HD), 1)

    @pl.when(valid > 0)
    def some():
        load_cache(valid, kv_ref, keys, values)
        stats = jnp.zeros((TOK, HD), jnp.float32)
        for at in range(STEP_HEADS):
            span = slice(at * HD, (at + 1) * HD)
            top, ext = over_cache(None, None, q_ref[:, span], keys, values)
            acc_ref[:, span] = ext[:, :HD]
            stats = jnp.where(lane == at, jnp.broadcast_to(top, (TOK, HD)), stats)
            stats = jnp.where(lane == at + STEP_HEADS, ext[:, HD:], stats)
        stat_ref[...] = stats

    @pl.when(valid <= 0)
    def none():
        acc_ref[...] = jnp.zeros_like(acc_ref)
        stat_ref[...] = jnp.where(lane < STEP_HEADS, LOW, 0.0)


def own_half(length, member, queries, cache, group, after, state=None):
    wide = STEP_HEADS * HD
    groups = HEADS // STEP_HEADS
    in_specs = [
        SMEM,
        SMEM,
        pl.BlockSpec((TOK, wide), lambda i: (0, group)),
        pl.BlockSpec((2, HALF, HD), lambda i: (0, 0, 0)),
        ANY,
    ]
    args = [length, member, queries, cache, after]
    aliases = {}
    if state is not None:
        aliases = {len(args): 0, len(args) + 1: 1}
        in_specs += [ANY, ANY]
        args += list(state)
    return pl.pallas_call(
        functools.partial(own_half_kernel, state is not None),
        grid=(1,),
        out_shape=[
            struct((TOK, HEADS * HD), jnp.float32),
            struct((TOK, groups * HD), jnp.float32),
        ],
        in_specs=in_specs,
        out_specs=[
            pl.BlockSpec((TOK, wide), lambda i: (0, group)),
            pl.BlockSpec((TOK, HD), lambda i: (0, group)),
        ],
        scratch_shapes=[
            pltpu.VMEM((HALF, HD), jnp.bfloat16),
            pltpu.VMEM((HALF, 2 * HD), jnp.bfloat16),
        ],
        input_output_aliases=aliases,
        compiler_params=params(24),
        cost_estimate=pl.CostEstimate(
            flops=8 * TOK * STEP_HEADS * HALF * HD,
            bytes_accessed=2 << 20,
            transcendentals=TOK * STEP_HEADS * HALF,
        ),
        name="own_half",
    )(*args)


def other_half_kernel(
    length_ref, member_ref, q_ref, kv_ref, acc_ref, stat_ref, mine_ref, theirs_ref,
    after_ref, out_ref, keys, values, new_keys, new_values,
):
    limit = length_ref[0] * BLOCK
    low = jnp.minimum(limit, HALF)
    is_key = member_ref[0] % 2 == 0
    valid = jnp.where(is_key, limit - low, low)
    lane = lax.broadcasted_iota(jnp.int32, (TOK, HD), 1)

    @pl.when(pl.program_id(0) == 0)
    def prepare():
        load_cache(valid, kv_ref, keys, values)
        new_keys[...] = jnp.where(is_key, mine_ref[...], theirs_ref[...])
        new_values[:, :HD] = jnp.where(is_key, theirs_ref[...], mine_ref[...])
        new_values[:, HD:] = jnp.ones((TOK, HD), jnp.bfloat16)

    def run(with_cache):
        stats = stat_ref[...]
        row = lax.broadcasted_iota(jnp.int32, (TOK, TOK), 0)
        column = lax.broadcasted_iota(jnp.int32, (TOK, TOK), 1)
        for at in range(STEP_HEADS):
            span = slice(at * HD, (at + 1) * HD)
            queried = q_ref[:, span]
            top = stats[:, at : at + 1]
            total = stats[:, at + STEP_HEADS : at + STEP_HEADS + 1]
            ext = jnp.concatenate(
                [acc_ref[:, span], jnp.broadcast_to(total, (TOK, HD))], axis=1
            )
            if with_cache:
                top, ext = over_cache(top, ext, queried, keys, values)
            scores = jnp.where(column <= row, dot_rows(queried, new_keys[...]), LOW)
            top, ext = update(top, ext, scores, new_values[...])
            out_ref[:, span] = (ext[:, :HD] / ext[:, HD:]).astype(jnp.bfloat16)

    pl.when(valid > 0)(lambda: run(True))
    pl.when(valid <= 0)(lambda: run(False))


def other_half(length, member, queries, cache, state, mine, theirs, after):
    wide = STEP_HEADS * HD
    heads_spec = pl.BlockSpec((TOK, wide), lambda g: (0, g))
    whole = pl.BlockSpec((TOK, HD), lambda g: (0, 0))
    return pl.pallas_call(
        other_half_kernel,
        grid=(HEADS // STEP_HEADS,),
        out_shape=struct((TOK, HEADS * HD), jnp.bfloat16),
        in_specs=[
            SMEM,
            SMEM,
            heads_spec,
            pl.BlockSpec((2, HALF, HD), lambda g: (0, 0, 0)),
            heads_spec,
            pl.BlockSpec((TOK, HD), lambda g: (0, g)),
            whole,
            whole,
            ANY,
        ],
        out_specs=heads_spec,
        scratch_shapes=[
            pltpu.VMEM((HALF, HD), jnp.bfloat16),
            pltpu.VMEM((HALF, 2 * HD), jnp.bfloat16),
            pltpu.VMEM((TOK, HD), jnp.bfloat16),
            pltpu.VMEM((TOK, 2 * HD), jnp.bfloat16),
        ],
        compiler_params=params(32),
        cost_estimate=pl.CostEstimate(
            flops=8 * TOK * HEADS * (HALF + TOK) * HD,
            bytes_accessed=3 << 20,
            transcendentals=TOK * HEADS * (HALF + TOK),
        ),
        name="other_half",
    )(length, member, queries, cache, *state, mine, theirs, after)


def rotation(length, is_key):
    half = HD // 2
    positions = (length * BLOCK + jnp.arange(TOK)).astype(jnp.float32)
    frequency = jnp.exp(jnp.arange(half).astype(jnp.float32) * (-2.0 * math.log(500000.0) / HD))
    angles = positions[:, None] * frequency[None, :]
    cosine = jnp.where(is_key, jnp.cos(angles), 1.0)
    sine = jnp.where(is_key, jnp.sin(angles), 0.0)
    return jnp.concatenate([cosine, cosine], 1), jnp.concatenate([-sine, sine], 1)


def per_device(hidden, queries, prefix_cache, lengths, pairing, w_kv):
    member = lax.axis_index("tp").astype(jnp.int32)
    inst = lax.axis_index("inst").astype(jnp.int32).reshape(1)
    role = lax.axis_index("role").astype(jnp.int32).reshape(1)
    length = lengths.reshape(1)
    resident = prefix_cache[0, 0, 0]
    queried = queries[0, 0]
    cosine, sine = rotation(lengths[0, 0], member % 2 == 0)
    member = member.reshape(1)

    own, *sends = project(member, hidden[0, 0], w_kv)
    with jax.named_scope("sum_x"):
        arrived = [swap_tp(sends[j - 1], j) for j in (1, 2, 3)]
    with jax.named_scope("prefix"):
        across = swap_tp(resident, 1)
    state = own_half(length, member, queried, resident, 0, sends[0])
    keep, *sends = sum_x(own, arrived, state[1])
    with jax.named_scope("sum_z"):
        arrived = [swap_tp(sends[k - 1], 4 * k) for k in (1, 2, 3)]
    state = own_half(length, member, queried, resident, 1, sends[0], state)
    own_kv = finish(keep, arrived, cosine, sine, state[1])

    with jax.named_scope("handoff_y"):
        column = [own_kv] + [
            role_inst(own_kv, [(i, i ^ j) for i in range(16)]) for j in (1, 2, 3)
        ]
    with jax.named_scope("pair"):
        other_kv = swap_tp(own_kv, 1)
    offers = offer(pairing, inst, column)
    with jax.named_scope("handoff_z"):
        offered = [
            role_inst(offers[j], [(i, 16 + (i ^ (4 * j))) for i in range(16)]) for j in range(4)
        ]
    attended = other_half(
        length, member, queried, across, state, own_kv, other_kv, offers[0]
    )
    layer_kv = take(pairing, inst, role, own_kv, offered, attended)
    return attended[None, None], layer_kv[None, None]


def solution(mesh):
    in_specs = (
        P("role", "inst", None, "tp"),
        P("role", "inst", None, "tp"),
        P("role", "inst", "tp", None, None, None),
        P("role", "inst"),
        P(),
        P("tp", None),
    )
    out_specs = (P("role", "inst", None, "tp"), P("role", "inst", None, "tp"))
    return jax.shard_map(
        per_device, mesh=mesh, in_specs=in_specs, out_specs=out_specs, check_vma=False
    )
```

```python
import functools
import math

import jax
import jax.numpy as jnp
from jax import lax
from jax.experimental import pallas as pl
from jax.experimental.pallas import tpu as pltpu
from jax.sharding import PartitionSpec as P

BLOCK = 128
HD = 128
TOK = 256
HALF = 2048
HEADS = 8
STEP_HEADS = 4
SUB = 512
FEATURES = 512
W_PARTS = 4
LOW = -1e30
SCALE = HD**-0.5 * math.log2(math.e)

SMEM = pl.BlockSpec(memory_space=pltpu.SMEM)
VMEM = pl.BlockSpec(memory_space=pltpu.VMEM)
HBM = pl.BlockSpec(memory_space=pltpu.HBM)
ANY = pl.BlockSpec(memory_space=pl.ANY)


def params(mib):
    return pltpu.CompilerParams(vmem_limit_bytes=mib * 1024 * 1024)


def struct(shape, dtype):
    return jax.ShapeDtypeStruct(shape, dtype)


TOKEN = struct((8, HD), jnp.float32)


def in_hbm(array):
    return pltpu.with_memory_space_constraint(array, pltpu.HBM)


def swap_tp(array, mask):
    return lax.ppermute(array, "tp", [(i, i ^ mask) for i in range(16)])


def role_inst(array, pairs):
    return lax.ppermute(array, ("role", "inst"), pairs)


def project_kernel(member_ref, hidden_hbm, w_hbm, own_ref, *rest):
    send_refs, token_ref, (hidden_ref, w_ref, sems) = rest[:3], rest[3], rest[4:]
    member = member_ref[0]
    rows = FEATURES // W_PARTS
    copies = [pltpu.make_async_copy(hidden_hbm, hidden_ref, sems.at[W_PARTS])]
    for part in range(W_PARTS):
        span = pl.ds(part * rows, rows)
        copies.append(pltpu.make_async_copy(w_hbm.at[span], w_ref.at[span], sems.at[part]))
    for copy in copies:
        copy.start()
    for copy in copies:
        copy.wait()
    for j in (2, 3, 1, 0):
        for k in range(4):
            column = pl.multiple_of((member ^ (4 * k + j)) * HD, HD)
            part = jnp.dot(
                hidden_ref[...], w_ref[:, pl.ds(column, HD)], preferred_element_type=jnp.float32
            )
            if j == 0:
                own_ref[k] = part
            else:
                send_refs[j - 1][k] = part.astype(jnp.bfloat16)
    token_ref[...] = jnp.zeros_like(token_ref)


def project(member, hidden, w_kv):
    return pl.pallas_call(
        project_kernel,
        out_shape=[struct((4, TOK, HD), jnp.float32)]
        + [struct((4, TOK, HD), jnp.bfloat16)] * 3
        + [TOKEN],
        in_specs=[SMEM, ANY, ANY],
        out_specs=[VMEM] * 5,
        scratch_shapes=[
            pltpu.VMEM((TOK, FEATURES), jnp.bfloat16),
            pltpu.VMEM((FEATURES, 2048), jnp.bfloat16),
            pltpu.SemaphoreType.DMA((W_PARTS + 1,)),
        ],
        compiler_params=params(12),
        cost_estimate=pl.CostEstimate(
            flops=2 * TOK * FEATURES * 2048, bytes_accessed=4 << 20, transcendentals=0
        ),
        name="project",
    )(member, in_hbm(hidden), in_hbm(w_kv))


def sum_x_kernel(own_ref, a_ref, b_ref, c_ref, after_ref, cache_ref, keep_ref, *refs):
    send_refs, (cache_out, sem) = refs[:3], refs[3:]
    copy = pltpu.make_async_copy(cache_ref, cache_out, sem)
    copy.start()
    for k in range(4):
        total = own_ref[k] + a_ref[k].astype(jnp.float32)
        total = total + b_ref[k].astype(jnp.float32) + c_ref[k].astype(jnp.float32)
        if k == 0:
            keep_ref[...] = total
        else:
            send_refs[k - 1][...] = total.astype(jnp.bfloat16)
    copy.wait()


def sum_x(own, arrived, after, cache):
    return pl.pallas_call(
        sum_x_kernel,
        out_shape=[struct((TOK, HD), jnp.float32)]
        + [struct((TOK, HD), jnp.bfloat16)] * 3
        + [struct(cache.shape, cache.dtype)],
        in_specs=[VMEM] * 5 + [ANY],
        out_specs=[VMEM] * 4 + [ANY],
        scratch_shapes=[pltpu.SemaphoreType.DMA],
        compiler_params=params(8),
        name="sum_x",
    )(own, *arrived, after, cache)


def finish_kernel(keep_ref, a_ref, b_ref, c_ref, cosine_ref, sine_ref, out_ref):
    total = keep_ref[...] + a_ref[...].astype(jnp.float32)
    total = total + b_ref[...].astype(jnp.float32) + c_ref[...].astype(jnp.float32)
    turned = pltpu.roll(total, HD // 2, 1)
    out_ref[...] = (total * cosine_ref[...] + turned * sine_ref[...]).astype(jnp.bfloat16)


def finish(keep, arrived, cosine, sine):
    return pl.pallas_call(
        finish_kernel,
        out_shape=struct((TOK, HD), jnp.bfloat16),
        in_specs=[VMEM] * 6,
        out_specs=VMEM,
        compiler_params=params(8),
        name="finish",
    )(keep, *arrived, cosine, sine)


def source_of(pairing_ref, target):
    source = jnp.int32(0)
    for i in range(16):
        source = jnp.where(pairing_ref[i] == target, i, source)
    return source


def choose(index, refs):
    block = refs[0][...]
    for at in range(1, len(refs)):
        block = jnp.where(index == at, refs[at][...], block)
    return block


def offer_kernel(pairing_ref, inst_ref, *refs):
    column, outs = refs[:4], refs[4:]
    inst = inst_ref[0]
    for j in range(4):
        source = source_of(pairing_ref, inst ^ (4 * j))
        outs[j][...] = choose((source ^ inst) & 3, column)


def offer(pairing, inst, column):
    return pl.pallas_call(
        offer_kernel,
        out_shape=[struct((TOK, HD), jnp.bfloat16)] * 4,
        in_specs=[SMEM] * 2 + [VMEM] * 4,
        out_specs=[VMEM] * 4,
        compiler_params=params(8),
        name="offer",
    )(pairing, inst, *column)


def dot_rows(a, b):
    return lax.dot_general(a, b, (((1,), (1,)), ((), ())), preferred_element_type=jnp.float32)


def load_cache(valid, kv_ref, keys, values):
    inside = lax.broadcasted_iota(jnp.int32, (HALF, HD), 0) < valid
    rows = kv_ref[0]
    keys[...] = jnp.where(inside, rows, jnp.broadcast_to(rows[:1], rows.shape))
    values[:, :HD] = jnp.where(inside, kv_ref[1], 0)
    values[:, HD:] = jnp.where(inside, 1.0, 0.0).astype(jnp.bfloat16)


def update(top, ext, scores, values):
    peak = jnp.max(scores, axis=1, keepdims=True) * SCALE
    if top is not None:
        peak = jnp.maximum(top, peak)
    weights = jnp.exp2(scores * SCALE - peak).astype(jnp.bfloat16)
    term = jnp.dot(weights, values, preferred_element_type=jnp.float32)
    if top is not None:
        term = ext * jnp.exp2(top - peak) + term
    return peak, term


def over_cache(top, ext, queried, keys, values):
    for at in range(0, HALF, SUB):
        scores = dot_rows(queried, keys[at : at + SUB, :])
        top, ext = update(top, ext, scores, values[at : at + SUB, :])
    return top, ext


def valid_slots(length_ref, member_ref):
    limit = length_ref[0] * BLOCK
    low = jnp.minimum(limit, HALF)
    is_key = member_ref[0] % 2 == 0
    return jnp.where(is_key, low, limit - low), jnp.where(is_key, limit - low, low), is_key


def own_half_kernel(
    length_ref, member_ref, q_ref, kv_ref, after_ref, acc_ref, stat_ref, token_ref, keys, values
):
    token_ref[...] = after_ref[...]
    valid, _, _ = valid_slots(length_ref, member_ref)
    lane = lax.broadcasted_iota(jnp.int32, (TOK, HD), 1)

    @pl.when((valid > 0) & (pl.program_id(0) == 0))
    def prepare():
        load_cache(valid, kv_ref, keys, values)

    @pl.when(valid > 0)
    def some():
        stats = jnp.zeros((TOK, HD), jnp.float32)
        for at in range(STEP_HEADS):
            span = slice(at * HD, (at + 1) * HD)
            top, ext = over_cache(None, None, q_ref[:, span], keys, values)
            acc_ref[:, span] = ext[:, :HD]
            stats = jnp.where(lane == at, jnp.broadcast_to(top, (TOK, HD)), stats)
            stats = jnp.where(lane == at + STEP_HEADS, ext[:, HD:], stats)
        stat_ref[...] = stats

    @pl.when(valid <= 0)
    def none():
        acc_ref[...] = jnp.zeros_like(acc_ref)
        stat_ref[...] = jnp.where(lane < STEP_HEADS, LOW, 0.0)


HEADS_SPEC = pl.BlockSpec((TOK, STEP_HEADS * HD), lambda g: (0, g))
STAT_SPEC = pl.BlockSpec((TOK, HD), lambda g: (0, g))
CACHE_SPEC = pl.BlockSpec((2, HALF, HD), lambda g: (0, 0, 0))
ROWS_SPEC = pl.BlockSpec((TOK, HD), lambda g: (0, 0))
TOKEN_SPEC = pl.BlockSpec((8, HD), lambda g: (0, 0))


def own_half(length, member, queries, cache, after):
    groups = HEADS // STEP_HEADS
    return pl.pallas_call(
        own_half_kernel,
        grid=(groups,),
        out_shape=[
            pltpu.HBM((TOK, HEADS * HD), jnp.float32),
            pltpu.HBM((TOK, groups * HD), jnp.float32),
            TOKEN,
        ],
        in_specs=[SMEM, SMEM, HEADS_SPEC, CACHE_SPEC, TOKEN_SPEC],
        out_specs=[HEADS_SPEC, STAT_SPEC, TOKEN_SPEC],
        scratch_shapes=[
            pltpu.VMEM((HALF, HD), jnp.bfloat16),
            pltpu.VMEM((HALF, 2 * HD), jnp.bfloat16),
        ],
        compiler_params=params(16),
        cost_estimate=pl.CostEstimate(
            flops=8 * TOK * HEADS * HALF * HD,
            bytes_accessed=2 << 20,
            transcendentals=TOK * HEADS * HALF,
        ),
        name="own_half",
    )(length, member, in_hbm(queries), in_hbm(cache), after)


def other_half_kernel(
    length_ref, member_ref, pairing_ref, inst_ref, role_ref, q_ref, kv_ref, acc_ref, stat_ref,
    mine_ref, theirs_ref, *refs,
):
    offers, (out_ref, layer_ref, keys, values, new_keys, new_values) = refs[:4], refs[4:]
    _, valid, is_key = valid_slots(length_ref, member_ref)

    @pl.when(pl.program_id(0) == 0)
    def prepare():
        inst = inst_ref[0]
        handed = choose((source_of(pairing_ref, inst) ^ inst) // 4, offers)
        layer_ref[...] = jnp.where(role_ref[0] == 1, handed, mine_ref[...])
        load_cache(valid, kv_ref, keys, values)
        new_keys[...] = jnp.where(is_key, mine_ref[...], theirs_ref[...])
        new_values[:, :HD] = jnp.where(is_key, theirs_ref[...], mine_ref[...])
        new_values[:, HD:] = jnp.ones((TOK, HD), jnp.bfloat16)

    def run(with_cache):
        row = lax.broadcasted_iota(jnp.int32, (TOK, TOK), 0)
        column = lax.broadcasted_iota(jnp.int32, (TOK, TOK), 1)
        for at in range(STEP_HEADS):
            span = slice(at * HD, (at + 1) * HD)
            queried = q_ref[:, span]
            scores = jnp.where(column <= row, dot_rows(queried, new_keys[...]), LOW)
            top, ext = update(None, None, scores, new_values[...])
            if with_cache:
                top, ext = over_cache(top, ext, queried, keys, values)
            own_top = stat_ref[:, at : at + 1]
            own_total = stat_ref[:, at + STEP_HEADS : at + STEP_HEADS + 1]
            peak = jnp.maximum(top, own_top)
            scale, own_scale = jnp.exp2(top - peak), jnp.exp2(own_top - peak)
            total = ext[:, HD:] * scale + own_total * own_scale
            out = ext[:, :HD] * scale + acc_ref[:, span] * own_scale
            out_ref[:, span] = (out / total).astype(jnp.bfloat16)

    pl.when(valid > 0)(lambda: run(True))
    pl.when(valid <= 0)(lambda: run(False))


def other_half(length, member, pairing, inst, role, queries, cache, state, mine, theirs, offers):
    return pl.pallas_call(
        other_half_kernel,
        grid=(HEADS // STEP_HEADS,),
        out_shape=[
            struct((TOK, HEADS * HD), jnp.bfloat16),
            struct((TOK, HD), jnp.bfloat16),
        ],
        in_specs=[SMEM] * 5
        + [HEADS_SPEC, CACHE_SPEC, HEADS_SPEC, STAT_SPEC]
        + [ROWS_SPEC] * 6,
        out_specs=[HEADS_SPEC, ROWS_SPEC],
        scratch_shapes=[
            pltpu.VMEM((HALF, HD), jnp.bfloat16),
            pltpu.VMEM((HALF, 2 * HD), jnp.bfloat16),
            pltpu.VMEM((TOK, HD), jnp.bfloat16),
            pltpu.VMEM((TOK, 2 * HD), jnp.bfloat16),
        ],
        compiler_params=params(24),
        cost_estimate=pl.CostEstimate(
            flops=8 * TOK * HEADS * (HALF + TOK) * HD,
            bytes_accessed=3 << 20,
            transcendentals=TOK * HEADS * (HALF + TOK),
        ),
        name="other_half",
    )(
        length, member, pairing, inst, role, in_hbm(queries), cache,
        in_hbm(state[0]), in_hbm(state[1]), mine, theirs, *offers,
    )


def rotation(length, is_key):
    half = HD // 2
    positions = (length * BLOCK + jnp.arange(TOK)).astype(jnp.float32)
    frequency = jnp.exp(jnp.arange(half).astype(jnp.float32) * (-2.0 * math.log(500000.0) / HD))
    angles = positions[:, None] * frequency[None, :]
    cosine = jnp.where(is_key, jnp.cos(angles), 1.0)
    sine = jnp.where(is_key, jnp.sin(angles), 0.0)
    return jnp.concatenate([cosine, cosine], 1), jnp.concatenate([-sine, sine], 1)


def per_device(hidden, queries, prefix_cache, lengths, pairing, w_kv):
    member = lax.axis_index("tp").astype(jnp.int32)
    inst = lax.axis_index("inst").astype(jnp.int32).reshape(1)
    role = lax.axis_index("role").astype(jnp.int32).reshape(1)
    length = lengths.reshape(1)
    resident = prefix_cache[0, 0, 0]
    queried = queries[0, 0]
    cosine, sine = rotation(lengths[0, 0], member % 2 == 0)
    member = member.reshape(1)

    own, *sends, token = project(member, hidden[0, 0], w_kv)
    with jax.named_scope("sum_x"):
        arrived = [swap_tp(sends[j - 1], j) for j in (1, 2, 3)]
    *state, token = own_half(length, member, queried, resident, token)
    keep, *sends, resend = sum_x(own, arrived, token, resident)
    with jax.named_scope("prefix"):
        across = swap_tp(resend, 1)
    with jax.named_scope("sum_z"):
        arrived = [swap_tp(sends[k - 1], 4 * k) for k in (1, 2, 3)]
    own_kv = finish(keep, arrived, cosine, sine)

    with jax.named_scope("handoff_y"):
        column = [own_kv] + [
            role_inst(own_kv, [(i, i ^ j) for i in range(16)]) for j in (1, 2, 3)
        ]
    with jax.named_scope("pair"):
        other_kv = swap_tp(own_kv, 1)
    offers = offer(pairing, inst, column)
    with jax.named_scope("handoff_z"):
        offered = [
            role_inst(offers[j], [(i, 16 + (i ^ (4 * j))) for i in range(16)]) for j in range(4)
        ]
    attended, layer_kv = other_half(
        length, member, pairing, inst, role, queried, across, state, own_kv, other_kv, offered
    )
    return attended[None, None], layer_kv[None, None]


def solution(mesh):
    in_specs = (
        P("role", "inst", None, "tp"),
        P("role", "inst", None, "tp"),
        P("role", "inst", "tp", None, None, None),
        P("role", "inst"),
        P(),
        P("tp", None),
    )
    out_specs = (P("role", "inst", None, "tp"), P("role", "inst", None, "tp"))
    return jax.shard_map(
        per_device, mesh=mesh, in_specs=in_specs, out_specs=out_specs, check_vma=False
    )
```

```python
import functools
import math

import jax
import jax.numpy as jnp
from jax import lax
from jax.experimental import pallas as pl
from jax.experimental.pallas import tpu as pltpu
from jax.sharding import PartitionSpec as P

BLOCK = 128
HD = 128
TOK = 256
HALF = 2048
HEADS = 8
STEP_HEADS = 4
SUB = 512
FEATURES = 512
LOW = -1e30
X_GROUPS = [[z * 4 + x for x in range(4)] for z in range(4)]
Y_GROUPS = [[zl * 4 + y for y in range(4)] for zl in range(4)]
Z_GROUPS = [[z * 4 + x for z in range(4)] for x in range(4)]
SCALE = HD**-0.5 * math.log2(math.e)

SMEM = pl.BlockSpec(memory_space=pltpu.SMEM)
VMEM = pl.BlockSpec(memory_space=pltpu.VMEM)
HBM = pl.BlockSpec(memory_space=pltpu.HBM)
ANY = pl.BlockSpec(memory_space=pl.ANY)


def params(mib):
    return pltpu.CompilerParams(vmem_limit_bytes=mib * 1024 * 1024)


def struct(shape, dtype):
    return jax.ShapeDtypeStruct(shape, dtype)


TOKEN = struct((8, HD), jnp.float32)


def in_hbm(array):
    return pltpu.with_memory_space_constraint(array, pltpu.HBM)


def swap_tp(array, mask):
    return lax.ppermute(array, "tp", [(i, i ^ mask) for i in range(16)])


def exchange_tp(array, groups):
    return lax.all_to_all(array, "tp", 0, 0, axis_index_groups=groups, tiled=True)


def role_inst(array, pairs):
    return lax.ppermute(array, ("role", "inst"), pairs)


def project_kernel(member_ref, hidden_hbm, w_hbm, send_ref, token_ref, hidden_ref, w_ref, sems):
    zh = member_ref[0] // 4
    width = 4 * HD
    copies = [pltpu.make_async_copy(hidden_hbm, hidden_ref, sems.at[4])]
    for k in range(4):
        column = pl.multiple_of((zh ^ k) * width, width)
        copies.append(
            pltpu.make_async_copy(w_hbm.at[:, pl.ds(column, width)], w_ref.at[k], sems.at[k])
        )
    for copy in copies:
        copy.start()
    copies[0].wait()
    token_ref[...] = jnp.zeros_like(token_ref)
    for k in range(4):
        copies[k + 1].wait()
        part = jnp.dot(hidden_ref[...], w_ref[k], preferred_element_type=jnp.float32)
        for x in range(4):
            send_ref[x, k] = part[:, x * HD : (x + 1) * HD].astype(jnp.bfloat16)


def project(member, hidden, w_kv):
    return pl.pallas_call(
        project_kernel,
        out_shape=[struct((4, 4, TOK, HD), jnp.bfloat16), TOKEN],
        in_specs=[SMEM, ANY, ANY],
        out_specs=[VMEM] * 2,
        scratch_shapes=[
            pltpu.VMEM((TOK, FEATURES), jnp.bfloat16),
            pltpu.VMEM((4, FEATURES, 4 * HD), jnp.bfloat16),
            pltpu.SemaphoreType.DMA((5,)),
        ],
        compiler_params=params(12),
        cost_estimate=pl.CostEstimate(
            flops=2 * TOK * FEATURES * 2048, bytes_accessed=4 << 20, transcendentals=0
        ),
        name="project",
    )(member, in_hbm(hidden), in_hbm(w_kv))


def sum_x_kernel(member_ref, parts_ref, after_ref, keep_ref, send_ref, token_ref):
    token_ref[...] = after_ref[...]
    zh = member_ref[0] // 4
    for k in range(4):
        total = parts_ref[0, k].astype(jnp.float32)
        for x in (1, 2, 3):
            total = total + parts_ref[x, k].astype(jnp.float32)
        if k == 0:
            keep_ref[...] = total
        send_ref[zh ^ k] = total.astype(jnp.bfloat16)


def sum_x(member, parts, after):
    return pl.pallas_call(
        sum_x_kernel,
        out_shape=[
            struct((TOK, HD), jnp.float32),
            struct((4, TOK, HD), jnp.bfloat16),
            TOKEN,
        ],
        in_specs=[SMEM] + [VMEM] * 2,
        out_specs=[VMEM] * 3,
        compiler_params=params(10),
        name="sum_x",
    )(member, parts, after)


def finish_kernel(member_ref, keep_ref, parts_ref, cosine_ref, sine_ref, after_ref, out_ref, send_ref):
    zh = member_ref[0] // 4
    total = keep_ref[...]
    for k in (1, 2, 3):
        total = total + parts_ref[zh ^ k].astype(jnp.float32)
    turned = pltpu.roll(total, HD // 2, 1)
    done = (total * cosine_ref[...] + turned * sine_ref[...]).astype(jnp.bfloat16)
    out_ref[...] = done
    for at in range(4):
        send_ref[at] = done


def finish(member, keep, parts, cosine, sine, after):
    return pl.pallas_call(
        finish_kernel,
        out_shape=[struct((TOK, HD), jnp.bfloat16), struct((4, TOK, HD), jnp.bfloat16)],
        in_specs=[SMEM] + [VMEM] * 5,
        out_specs=[VMEM] * 2,
        compiler_params=params(8),
        name="finish",
    )(member, keep, parts, cosine, sine, after)


def source_of(pairing_ref, target):
    source = jnp.int32(0)
    for i in range(16):
        source = jnp.where(pairing_ref[i] == target, i, source)
    return source


def choose(index, refs):
    block = refs[0][...]
    for at in range(1, len(refs)):
        block = jnp.where(index == at, refs[at][...], block)
    return block


def offer_kernel(pairing_ref, inst_ref, *refs):
    column, outs = refs[0], refs[1:]
    inst = inst_ref[0]
    for j in range(4):
        source = source_of(pairing_ref, inst ^ (4 * j))
        outs[j][...] = column[source & 3]


def offer(pairing, inst, column):
    return pl.pallas_call(
        offer_kernel,
        out_shape=[struct((TOK, HD), jnp.bfloat16)] * 4,
        in_specs=[SMEM] * 2 + [VMEM],
        out_specs=[VMEM] * 4,
        compiler_params=params(8),
        name="offer",
    )(pairing, inst, column)


def take_kernel(pairing_ref, inst_ref, role_ref, own_ref, *refs):
    offers, out_ref = refs[:4], refs[5]
    inst = inst_ref[0]
    handed = choose((source_of(pairing_ref, inst) ^ inst) // 4, offers)
    out_ref[...] = jnp.where(role_ref[0] == 1, handed, own_ref[...])


def take(pairing, inst, role, own_kv, offers, after):
    return pl.pallas_call(
        take_kernel,
        out_shape=struct((TOK, HD), jnp.bfloat16),
        in_specs=[SMEM] * 3 + [VMEM] * 6,
        out_specs=VMEM,
        compiler_params=params(8),
        name="take",
    )(pairing, inst, role, own_kv, *offers, after)


def dot_rows(a, b):
    return lax.dot_general(a, b, (((1,), (1,)), ((), ())), preferred_element_type=jnp.float32)


def load_cache(valid, kv_ref, keys, values):
    inside = lax.broadcasted_iota(jnp.int32, keys.shape, 0) < valid
    rows = kv_ref[0]
    keys[...] = jnp.where(inside, rows, jnp.broadcast_to(rows[:1], rows.shape))
    values[:, :HD] = jnp.where(inside, kv_ref[1], 0)
    values[:, HD:] = jnp.where(inside, 1.0, 0.0).astype(jnp.bfloat16)


def update(top, ext, scores, values):
    peak = jnp.max(scores, axis=1, keepdims=True) * SCALE
    if top is not None:
        peak = jnp.maximum(top, peak)
    weights = jnp.exp2(scores * SCALE - peak).astype(jnp.bfloat16)
    term = jnp.dot(weights, values, preferred_element_type=jnp.float32)
    if top is not None:
        term = ext * jnp.exp2(top - peak) + term
    return peak, term


def over_cache(top, ext, queried, keys, values):
    for at in range(0, keys.shape[0], SUB):
        scores = dot_rows(queried, keys[at : at + SUB, :])
        top, ext = update(top, ext, scores, values[at : at + SUB, :])
    return top, ext


def merge(state, other):
    (top, total, acc), (other_top, other_total, other_acc) = state, other
    peak = jnp.maximum(top, other_top)
    scale, other_scale = jnp.exp2(top - peak), jnp.exp2(other_top - peak)
    return peak, total * scale + other_total * other_scale, acc * scale + other_acc * other_scale


def valid_slots(length_ref, member_ref, own, at, count):
    limit = length_ref[0] * BLOCK
    low = jnp.minimum(limit, HALF)
    first_half = (member_ref[0] % 2 == 0) == own
    return jnp.clip(jnp.where(first_half, low, limit - low) - at, 0, count)


def cache_part_kernel(own, at_slot, length_ref, member_ref, q_ref, kv_ref, after_ref, *refs):
    if own:
        before, (top_ref, total_ref, acc_ref, token_ref, chunk_ref, keys, values) = (), refs

        @pl.when(pl.program_id(0) == 0)
        def pass_on():
            chunk_ref[...] = kv_ref[:, : chunk_ref.shape[1], :]

    else:
        before, (top_ref, total_ref, acc_ref, token_ref, keys, values) = refs[:3], refs[3:]
    valid = valid_slots(length_ref, member_ref, own, at_slot, keys.shape[0])

    @pl.when(pl.program_id(0) == 0)
    def prepare():
        token_ref[...] = after_ref[...]
        load_cache(valid, kv_ref, keys, values)

    @pl.when(valid > 0)
    def some():
        for at in range(STEP_HEADS):
            span = slice(at * HD, (at + 1) * HD)
            top, ext = over_cache(None, None, q_ref[:, span], keys, values)
            state = jnp.broadcast_to(top, (TOK, HD)), ext[:, HD:], ext[:, :HD]
            if before:
                state = merge(state, [ref[:, span] for ref in before])
            top_ref[:, span], total_ref[:, span], acc_ref[:, span] = state

    @pl.when(valid <= 0)
    def none():
        for at, ref in enumerate((top_ref, total_ref, acc_ref)):
            ref[...] = before[at][...] if before else jnp.full(ref.shape, 0.0 if at else LOW)


HEADS_SPEC = pl.BlockSpec((TOK, STEP_HEADS * HD), lambda g: (0, g))
ROWS_SPEC = pl.BlockSpec((TOK, HD), lambda g: (0, 0))
TOKEN_SPEC = pl.BlockSpec((8, HD), lambda g: (0, 0))


def cache_part(length, member, queries, cache, after, own, at, state=()):
    count = cache.shape[1]
    return pl.pallas_call(
        functools.partial(cache_part_kernel, own, at),
        grid=(HEADS // STEP_HEADS,),
        out_shape=[pltpu.HBM((TOK, HEADS * HD), jnp.float32)] * 3
        + [TOKEN]
        + [struct((2, HALF, HD), jnp.bfloat16)] * own,
        in_specs=[
            SMEM, SMEM, HEADS_SPEC, pl.BlockSpec(cache.shape, lambda g: (0, 0, 0)), TOKEN_SPEC,
        ]
        + [HEADS_SPEC] * len(state),
        out_specs=[HEADS_SPEC] * 3
        + [TOKEN_SPEC]
        + [pl.BlockSpec((2, HALF, HD), lambda g: (0, 0, 0))] * own,
        scratch_shapes=[
            pltpu.VMEM((count, HD), jnp.bfloat16),
            pltpu.VMEM((count, 2 * HD), jnp.bfloat16),
        ],
        compiler_params=params(20),
        cost_estimate=pl.CostEstimate(
            flops=8 * TOK * HEADS * count * HD,
            bytes_accessed=2 << 20,
            transcendentals=TOK * HEADS * count,
        ),
        name="own_half" if own else "other_part",
    )(length, member, in_hbm(queries), cache, after, *(in_hbm(part) for part in state))


def last_kernel(length_ref, member_ref, q_ref, kv_ref, *refs):
    before, (mine_ref, theirs_ref) = refs[:3], refs[3:5]
    out_ref, token_ref, keys, values, new_keys, new_values = refs[5:]
    is_key = member_ref[0] % 2 == 0
    valid = valid_slots(length_ref, member_ref, False, 0, HALF)

    @pl.when(pl.program_id(0) == 0)
    def prepare():
        token_ref[...] = jnp.zeros_like(token_ref)
        load_cache(valid, kv_ref, keys, values)
        new_keys[...] = jnp.where(is_key, mine_ref[...], theirs_ref[...])
        new_values[:, :HD] = jnp.where(is_key, theirs_ref[...], mine_ref[...])
        new_values[:, HD:] = jnp.ones((TOK, HD), jnp.bfloat16)

    def run(with_cache):
        row = lax.broadcasted_iota(jnp.int32, (TOK, TOK), 0)
        column = lax.broadcasted_iota(jnp.int32, (TOK, TOK), 1)
        for at in range(STEP_HEADS):
            span = slice(at * HD, (at + 1) * HD)
            queried = q_ref[:, span]
            scores = jnp.where(column <= row, dot_rows(queried, new_keys[...]), LOW)
            top, ext = update(None, None, scores, new_values[...])
            if with_cache:
                top, ext = over_cache(top, ext, queried, keys, values)
            state = jnp.broadcast_to(top, (TOK, HD)), ext[:, HD:], ext[:, :HD]
            _, total, acc = merge(state, [ref[:, span] for ref in before])
            out_ref[:, span] = (acc / total).astype(jnp.bfloat16)

    pl.when(valid > 0)(lambda: run(True))
    pl.when(valid <= 0)(lambda: run(False))


def last(length, member, queries, cache, state, mine, theirs):
    slots = HALF + TOK
    return pl.pallas_call(
        last_kernel,
        grid=(HEADS // STEP_HEADS,),
        out_shape=[struct((TOK, HEADS * HD), jnp.bfloat16), TOKEN],
        in_specs=[SMEM] * 2
        + [HEADS_SPEC, pl.BlockSpec(cache.shape, lambda g: (0, 0, 0))]
        + [HEADS_SPEC] * 3
        + [ROWS_SPEC] * 2,
        out_specs=[HEADS_SPEC, TOKEN_SPEC],
        scratch_shapes=[
            pltpu.VMEM((HALF, HD), jnp.bfloat16),
            pltpu.VMEM((HALF, 2 * HD), jnp.bfloat16),
            pltpu.VMEM((TOK, HD), jnp.bfloat16),
            pltpu.VMEM((TOK, 2 * HD), jnp.bfloat16),
        ],
        compiler_params=params(24),
        cost_estimate=pl.CostEstimate(
            flops=8 * TOK * HEADS * slots * HD,
            bytes_accessed=3 << 20,
            transcendentals=TOK * HEADS * slots,
        ),
        name="last",
    )(
        length, member, in_hbm(queries), cache, *(in_hbm(part) for part in state), mine, theirs,
    )


def rotation(length, is_key):
    half = HD // 2
    positions = (length * BLOCK + jnp.arange(TOK)).astype(jnp.float32)
    frequency = jnp.exp(jnp.arange(half).astype(jnp.float32) * (-2.0 * math.log(500000.0) / HD))
    angles = positions[:, None] * frequency[None, :]
    cosine = jnp.where(is_key, jnp.cos(angles), 1.0)
    sine = jnp.where(is_key, jnp.sin(angles), 0.0)
    return jnp.concatenate([cosine, cosine], 1), jnp.concatenate([-sine, sine], 1)


def per_device(hidden, queries, prefix_cache, lengths, pairing, w_kv):
    member = lax.axis_index("tp").astype(jnp.int32)
    inst = lax.axis_index("inst").astype(jnp.int32).reshape(1)
    role = lax.axis_index("role").astype(jnp.int32).reshape(1)
    length = lengths.reshape(1)
    resident = prefix_cache[0, 0, 0]
    queried = queries[0, 0]
    cosine, sine = rotation(lengths[0, 0], member % 2 == 0)
    member = member.reshape(1)

    parts, token = project(member, hidden[0, 0], w_kv)
    with jax.named_scope("sum_x"):
        parts = exchange_tp(parts, X_GROUPS)
    *state, token, chunk = cache_part(length, member, queried, in_hbm(resident), token, True, 0)
    with jax.named_scope("prefix_first"):
        across = swap_tp(chunk, 1)
    keep, parts, token = sum_x(member, parts, token)
    with jax.named_scope("sum_z"):
        parts = exchange_tp(parts, Z_GROUPS)
    own_kv, sends = finish(member, keep, parts, cosine, sine, token)

    with jax.named_scope("handoff_y"):
        column = lax.all_to_all(
            sends, "inst", 0, 0, axis_index_groups=Y_GROUPS, tiled=True
        )
    with jax.named_scope("pair"):
        other_kv = swap_tp(own_kv, 1)
    offers = offer(pairing, inst, column)
    with jax.named_scope("handoff_z"):
        offered = [
            role_inst(offers[j], [(i, 16 + (i ^ (4 * j))) for i in range(16)]) for j in range(4)
        ]
    attended, token = last(length, member, queried, across, state, own_kv, other_kv)
    layer_kv = take(pairing, inst, role, own_kv, offered, token)
    return attended[None, None], layer_kv[None, None]


def solution(mesh):
    in_specs = (
        P("role", "inst", None, "tp"),
        P("role", "inst", None, "tp"),
        P("role", "inst", "tp", None, None, None),
        P("role", "inst"),
        P(),
        P("tp", None),
    )
    out_specs = (P("role", "inst", None, "tp"), P("role", "inst", None, "tp"))
    return jax.shard_map(
        per_device, mesh=mesh, in_specs=in_specs, out_specs=out_specs, check_vma=False
    )
```

```python
import functools
import math

import jax
import jax.numpy as jnp
from jax import lax
from jax.experimental import pallas as pl
from jax.experimental.pallas import tpu as pltpu
from jax.sharding import PartitionSpec as P

BLOCK = 128
HD = 128
TOK = 256
HALF = 2048
HEADS = 8
STEP_HEADS = 4
SUB = 512
FEATURES = 512
LOW = -1e30
X_GROUPS = [[z * 4 + x for x in range(4)] for z in range(4)]
Y_GROUPS = [[zl * 4 + y for y in range(4)] for zl in range(4)]
Z_GROUPS = [[z * 4 + x for z in range(4)] for x in range(4)]
SCALE = HD**-0.5 * math.log2(math.e)

SMEM = pl.BlockSpec(memory_space=pltpu.SMEM)
VMEM = pl.BlockSpec(memory_space=pltpu.VMEM)
HBM = pl.BlockSpec(memory_space=pltpu.HBM)
ANY = pl.BlockSpec(memory_space=pl.ANY)


def params(mib):
    return pltpu.CompilerParams(vmem_limit_bytes=mib * 1024 * 1024)


def struct(shape, dtype):
    return jax.ShapeDtypeStruct(shape, dtype)


TOKEN = struct((8, HD), jnp.float32)


def in_hbm(array):
    return pltpu.with_memory_space_constraint(array, pltpu.HBM)


def swap_tp(array, mask):
    return lax.ppermute(array, "tp", [(i, i ^ mask) for i in range(16)])


def exchange_tp(array, groups):
    return lax.all_to_all(array, "tp", 0, 0, axis_index_groups=groups, tiled=True)


def role_inst(array, pairs):
    return lax.ppermute(array, ("role", "inst"), pairs)


def project_kernel(member_ref, hidden_hbm, w_hbm, send_ref, token_ref, hidden_ref, w_ref, sems):
    zh = member_ref[0] // 4
    width = 4 * HD
    copies = [pltpu.make_async_copy(hidden_hbm, hidden_ref, sems.at[4])]
    for k in range(4):
        column = pl.multiple_of((zh ^ k) * width, width)
        copies.append(
            pltpu.make_async_copy(w_hbm.at[:, pl.ds(column, width)], w_ref.at[k], sems.at[k])
        )
    for copy in copies:
        copy.start()
    copies[0].wait()
    token_ref[...] = jnp.zeros_like(token_ref)
    for k in range(4):
        copies[k + 1].wait()
        part = jnp.dot(hidden_ref[...], w_ref[k], preferred_element_type=jnp.float32)
        for x in range(4):
            send_ref[x, k] = part[:, x * HD : (x + 1) * HD].astype(jnp.bfloat16)


def project(member, hidden, w_kv):
    return pl.pallas_call(
        project_kernel,
        out_shape=[struct((4, 4, TOK, HD), jnp.bfloat16), TOKEN],
        in_specs=[SMEM, ANY, ANY],
        out_specs=[VMEM] * 2,
        scratch_shapes=[
            pltpu.VMEM((TOK, FEATURES), jnp.bfloat16),
            pltpu.VMEM((4, FEATURES, 4 * HD), jnp.bfloat16),
            pltpu.SemaphoreType.DMA((5,)),
        ],
        compiler_params=params(12),
        cost_estimate=pl.CostEstimate(
            flops=2 * TOK * FEATURES * 2048, bytes_accessed=4 << 20, transcendentals=0
        ),
        name="project",
    )(member, in_hbm(hidden), in_hbm(w_kv))


def sum_x_kernel(member_ref, parts_ref, after_ref, keep_ref, send_ref, token_ref):
    token_ref[...] = after_ref[...]
    zh = member_ref[0] // 4
    for k in range(4):
        total = parts_ref[0, k].astype(jnp.float32)
        for x in (1, 2, 3):
            total = total + parts_ref[x, k].astype(jnp.float32)
        if k == 0:
            keep_ref[...] = total
        send_ref[zh ^ k] = total.astype(jnp.bfloat16)


def sum_x(member, parts, after):
    return pl.pallas_call(
        sum_x_kernel,
        out_shape=[
            struct((TOK, HD), jnp.float32),
            struct((4, TOK, HD), jnp.bfloat16),
            TOKEN,
        ],
        in_specs=[SMEM] + [VMEM] * 2,
        out_specs=[VMEM] * 3,
        compiler_params=params(10),
        name="sum_x",
    )(member, parts, after)


def finish_kernel(member_ref, keep_ref, parts_ref, cosine_ref, sine_ref, after_ref, out_ref, send_ref):
    zh = member_ref[0] // 4
    total = keep_ref[...]
    for k in (1, 2, 3):
        total = total + parts_ref[zh ^ k].astype(jnp.float32)
    turned = pltpu.roll(total, HD // 2, 1)
    done = (total * cosine_ref[...] + turned * sine_ref[...]).astype(jnp.bfloat16)
    out_ref[...] = done
    for at in range(4):
        send_ref[at] = done


def finish(member, keep, parts, cosine, sine, after):
    return pl.pallas_call(
        finish_kernel,
        out_shape=[struct((TOK, HD), jnp.bfloat16), struct((4, TOK, HD), jnp.bfloat16)],
        in_specs=[SMEM] + [VMEM] * 5,
        out_specs=[VMEM] * 2,
        compiler_params=params(8),
        name="finish",
    )(member, keep, parts, cosine, sine, after)


def source_of(pairing_ref, target):
    source = jnp.int32(0)
    for i in range(16):
        source = jnp.where(pairing_ref[i] == target, i, source)
    return source


def choose(index, refs):
    block = refs[0][...]
    for at in range(1, len(refs)):
        block = jnp.where(index == at, refs[at][...], block)
    return block


def offer_kernel(pairing_ref, inst_ref, *refs):
    column, outs = refs[0], refs[1:]
    inst = inst_ref[0]
    for j in range(4):
        source = source_of(pairing_ref, inst ^ (4 * j))
        outs[j][...] = column[source & 3]


def offer(pairing, inst, column):
    return pl.pallas_call(
        offer_kernel,
        out_shape=[struct((TOK, HD), jnp.bfloat16)] * 4,
        in_specs=[SMEM] * 2 + [VMEM],
        out_specs=[VMEM] * 4,
        compiler_params=params(8),
        name="offer",
    )(pairing, inst, column)


def take_kernel(pairing_ref, inst_ref, role_ref, own_ref, *refs):
    offers, out_ref = refs[:4], refs[5]
    inst = inst_ref[0]
    handed = choose((source_of(pairing_ref, inst) ^ inst) // 4, offers)
    out_ref[...] = jnp.where(role_ref[0] == 1, handed, own_ref[...])


def take(pairing, inst, role, own_kv, offers, after):
    return pl.pallas_call(
        take_kernel,
        out_shape=struct((TOK, HD), jnp.bfloat16),
        in_specs=[SMEM] * 3 + [VMEM] * 6,
        out_specs=VMEM,
        compiler_params=params(8),
        name="take",
    )(pairing, inst, role, own_kv, *offers, after)


def dot_rows(a, b):
    return lax.dot_general(a, b, (((1,), (1,)), ((), ())), preferred_element_type=jnp.float32)


def load_cache(valid, kv_ref, keys, values):
    inside = lax.broadcasted_iota(jnp.int32, keys.shape, 0) < valid
    rows = kv_ref[0]
    keys[...] = jnp.where(inside, rows, jnp.broadcast_to(rows[:1], rows.shape))
    values[:, :HD] = jnp.where(inside, kv_ref[1], 0)
    values[:, HD:] = jnp.where(inside, 1.0, 0.0).astype(jnp.bfloat16)


def update(top, ext, scores, values):
    peak = jnp.max(scores, axis=1, keepdims=True) * SCALE
    if top is not None:
        peak = jnp.maximum(top, peak)
    weights = jnp.exp2(scores * SCALE - peak).astype(jnp.bfloat16)
    term = jnp.dot(weights, values, preferred_element_type=jnp.float32)
    if top is not None:
        term = ext * jnp.exp2(top - peak) + term
    return peak, term


def over_cache(top, ext, queried, keys, values):
    for at in range(0, keys.shape[0], SUB):
        scores = dot_rows(queried, keys[at : at + SUB, :])
        top, ext = update(top, ext, scores, values[at : at + SUB, :])
    return top, ext


def merge(state, other):
    (top, total, acc), (other_top, other_total, other_acc) = state, other
    peak = jnp.maximum(top, other_top)
    scale, other_scale = jnp.exp2(top - peak), jnp.exp2(other_top - peak)
    return peak, total * scale + other_total * other_scale, acc * scale + other_acc * other_scale


def valid_slots(length_ref, member_ref, own, at, count):
    limit = length_ref[0] * BLOCK
    low = jnp.minimum(limit, HALF)
    first_half = (member_ref[0] % 2 == 0) == own
    return jnp.clip(jnp.where(first_half, low, limit - low) - at, 0, count)


def cache_part_kernel(own, at_slot, length_ref, member_ref, q_ref, kv_ref, after_ref, *refs):
    if own:
        before, (top_ref, total_ref, acc_ref, token_ref, chunk_ref, keys, values) = (), refs

        @pl.when(pl.program_id(0) == 0)
        def pass_on():
            chunk_ref[...] = kv_ref[:, : chunk_ref.shape[1], :]

    else:
        before, (top_ref, total_ref, acc_ref, token_ref, keys, values) = refs[:3], refs[3:]
    valid = valid_slots(length_ref, member_ref, own, at_slot, keys.shape[0])

    @pl.when(pl.program_id(0) == 0)
    def prepare():
        token_ref[...] = after_ref[...]
        load_cache(valid, kv_ref, keys, values)

    @pl.when(valid > 0)
    def some():
        for at in range(STEP_HEADS):
            span = slice(at * HD, (at + 1) * HD)
            top, ext = over_cache(None, None, q_ref[:, span], keys, values)
            state = jnp.broadcast_to(top, (TOK, HD)), ext[:, HD:], ext[:, :HD]
            if before:
                state = merge(state, [ref[:, span] for ref in before])
            top_ref[:, span], total_ref[:, span], acc_ref[:, span] = state

    @pl.when(valid <= 0)
    def none():
        for at, ref in enumerate((top_ref, total_ref, acc_ref)):
            ref[...] = before[at][...] if before else jnp.full(ref.shape, 0.0 if at else LOW)


HEADS_SPEC = pl.BlockSpec((TOK, STEP_HEADS * HD), lambda g: (0, g))
ROWS_SPEC = pl.BlockSpec((TOK, HD), lambda g: (0, 0))
TOKEN_SPEC = pl.BlockSpec((8, HD), lambda g: (0, 0))


def cache_part(length, member, queries, cache, after, own, at, state=()):
    count = cache.shape[1]
    return pl.pallas_call(
        functools.partial(cache_part_kernel, own, at),
        grid=(HEADS // STEP_HEADS,),
        out_shape=[pltpu.HBM((TOK, HEADS * HD), jnp.float32)] * 3
        + [TOKEN]
        + [struct((2, HALF, HD), jnp.bfloat16)] * own,
        in_specs=[
            SMEM, SMEM, HEADS_SPEC, pl.BlockSpec(cache.shape, lambda g: (0, 0, 0)), TOKEN_SPEC,
        ]
        + [HEADS_SPEC] * len(state),
        out_specs=[HEADS_SPEC] * 3
        + [TOKEN_SPEC]
        + [pl.BlockSpec((2, HALF, HD), lambda g: (0, 0, 0))] * own,
        scratch_shapes=[
            pltpu.VMEM((count, HD), jnp.bfloat16),
            pltpu.VMEM((count, 2 * HD), jnp.bfloat16),
        ],
        compiler_params=params(20),
        cost_estimate=pl.CostEstimate(
            flops=8 * TOK * HEADS * count * HD,
            bytes_accessed=2 << 20,
            transcendentals=TOK * HEADS * count,
        ),
        name="own_half" if own else "other_part",
    )(length, member, in_hbm(queries), cache, after, *(in_hbm(part) for part in state))


def last_kernel(member_ref, q_ref, *refs):
    before, (mine_ref, theirs_ref) = refs[:3], refs[3:5]
    out_ref, token_ref, new_keys, new_values = refs[5:]
    is_key = member_ref[0] % 2 == 0

    @pl.when(pl.program_id(0) == 0)
    def prepare():
        token_ref[...] = jnp.zeros_like(token_ref)
        new_keys[...] = jnp.where(is_key, mine_ref[...], theirs_ref[...])
        new_values[:, :HD] = jnp.where(is_key, theirs_ref[...], mine_ref[...])
        new_values[:, HD:] = jnp.ones((TOK, HD), jnp.bfloat16)

    row = lax.broadcasted_iota(jnp.int32, (TOK, TOK), 0)
    column = lax.broadcasted_iota(jnp.int32, (TOK, TOK), 1)
    for at in range(STEP_HEADS):
        span = slice(at * HD, (at + 1) * HD)
        scores = jnp.where(column <= row, dot_rows(q_ref[:, span], new_keys[...]), LOW)
        top, ext = update(None, None, scores, new_values[...])
        state = jnp.broadcast_to(top, (TOK, HD)), ext[:, HD:], ext[:, :HD]
        _, total, acc = merge(state, [ref[:, span] for ref in before])
        out_ref[:, span] = (acc / total).astype(jnp.bfloat16)


def last(member, queries, state, mine, theirs):
    return pl.pallas_call(
        last_kernel,
        grid=(HEADS // STEP_HEADS,),
        out_shape=[struct((TOK, HEADS * HD), jnp.bfloat16), TOKEN],
        in_specs=[SMEM] + [HEADS_SPEC] * 4 + [ROWS_SPEC] * 2,
        out_specs=[HEADS_SPEC, TOKEN_SPEC],
        scratch_shapes=[
            pltpu.VMEM((TOK, HD), jnp.bfloat16),
            pltpu.VMEM((TOK, 2 * HD), jnp.bfloat16),
        ],
        compiler_params=params(16),
        cost_estimate=pl.CostEstimate(
            flops=8 * TOK * HEADS * TOK * HD,
            bytes_accessed=3 << 20,
            transcendentals=TOK * HEADS * TOK,
        ),
        name="last",
    )(member, in_hbm(queries), *(in_hbm(part) for part in state), mine, theirs)


def rotation(length, is_key):
    half = HD // 2
    positions = (length * BLOCK + jnp.arange(TOK)).astype(jnp.float32)
    frequency = jnp.exp(jnp.arange(half).astype(jnp.float32) * (-2.0 * math.log(500000.0) / HD))
    angles = positions[:, None] * frequency[None, :]
    cosine = jnp.where(is_key, jnp.cos(angles), 1.0)
    sine = jnp.where(is_key, jnp.sin(angles), 0.0)
    return jnp.concatenate([cosine, cosine], 1), jnp.concatenate([-sine, sine], 1)


def per_device(hidden, queries, prefix_cache, lengths, pairing, w_kv):
    member = lax.axis_index("tp").astype(jnp.int32)
    inst = lax.axis_index("inst").astype(jnp.int32).reshape(1)
    role = lax.axis_index("role").astype(jnp.int32).reshape(1)
    length = lengths.reshape(1)
    resident = prefix_cache[0, 0, 0]
    queried = queries[0, 0]
    cosine, sine = rotation(lengths[0, 0], member % 2 == 0)
    member = member.reshape(1)

    parts, token = project(member, hidden[0, 0], w_kv)
    with jax.named_scope("sum_x"):
        parts = exchange_tp(parts, X_GROUPS)
    *state, token, chunk = cache_part(length, member, queried, in_hbm(resident), token, True, 0)
    with jax.named_scope("prefix_first"):
        across = swap_tp(chunk, 1)
    keep, parts, token = sum_x(member, parts, token)
    with jax.named_scope("sum_z"):
        parts = exchange_tp(parts, Z_GROUPS)
    *state, token = cache_part(length, member, queried, across, token, False, 0, state)
    own_kv, sends = finish(member, keep, parts, cosine, sine, token)

    with jax.named_scope("handoff_y"):
        column = lax.all_to_all(
            sends, "inst", 0, 0, axis_index_groups=Y_GROUPS, tiled=True
        )
    with jax.named_scope("pair"):
        other_kv = swap_tp(own_kv, 1)
    offers = offer(pairing, inst, column)
    with jax.named_scope("handoff_z"):
        offered = [
            role_inst(offers[j], [(i, 16 + (i ^ (4 * j))) for i in range(16)]) for j in range(4)
        ]
    attended, token = last(member, queried, state, own_kv, other_kv)
    layer_kv = take(pairing, inst, role, own_kv, offered, token)
    return attended[None, None], layer_kv[None, None]


def solution(mesh):
    in_specs = (
        P("role", "inst", None, "tp"),
        P("role", "inst", None, "tp"),
        P("role", "inst", "tp", None, None, None),
        P("role", "inst"),
        P(),
        P("tp", None),
    )
    out_specs = (P("role", "inst", None, "tp"), P("role", "inst", None, "tp"))
    return jax.shard_map(
        per_device, mesh=mesh, in_specs=in_specs, out_specs=out_specs, check_vma=False
    )
```

```python
import functools
import math

import jax
import jax.numpy as jnp
from jax import lax
from jax.experimental import pallas as pl
from jax.experimental.pallas import tpu as pltpu
from jax.sharding import PartitionSpec as P

BLOCK = 128
HD = 128
TOK = 256
HALF = 2048
HEADS = 8
STEP_HEADS = 4
SUB = 512
FEATURES = 512
LOW = -1e30
X_GROUPS = [[z * 4 + x for x in range(4)] for z in range(4)]
Y_GROUPS = [[zl * 4 + y for y in range(4)] for zl in range(4)]
Z_GROUPS = [[z * 4 + x for z in range(4)] for x in range(4)]
SCALE = HD**-0.5 * math.log2(math.e)

SMEM = pl.BlockSpec(memory_space=pltpu.SMEM)
VMEM = pl.BlockSpec(memory_space=pltpu.VMEM)
HBM = pl.BlockSpec(memory_space=pltpu.HBM)
ANY = pl.BlockSpec(memory_space=pl.ANY)


def params(mib):
    return pltpu.CompilerParams(vmem_limit_bytes=mib * 1024 * 1024)


def struct(shape, dtype):
    return jax.ShapeDtypeStruct(shape, dtype)


TOKEN = struct((8, HD), jnp.float32)


def in_hbm(array):
    return pltpu.with_memory_space_constraint(array, pltpu.HBM)


def swap_tp(array, mask):
    return lax.ppermute(array, "tp", [(i, i ^ mask) for i in range(16)])


def exchange_tp(array, groups):
    return lax.all_to_all(array, "tp", 0, 0, axis_index_groups=groups, tiled=True)


def role_inst(array, pairs):
    return lax.ppermute(array, ("role", "inst"), pairs)


def project_kernel(member_ref, hidden_hbm, w_hbm, send_ref, token_ref, hidden_ref, w_ref, sems):
    zh = member_ref[0] // 4
    width = 4 * HD
    copies = [pltpu.make_async_copy(hidden_hbm, hidden_ref, sems.at[4])]
    for k in range(4):
        column = pl.multiple_of((zh ^ k) * width, width)
        copies.append(
            pltpu.make_async_copy(w_hbm.at[:, pl.ds(column, width)], w_ref.at[k], sems.at[k])
        )
    for copy in copies:
        copy.start()
    copies[0].wait()
    token_ref[...] = jnp.zeros_like(token_ref)
    for k in range(4):
        copies[k + 1].wait()
        part = jnp.dot(hidden_ref[...], w_ref[k], preferred_element_type=jnp.float32)
        for x in range(4):
            send_ref[x, k] = part[:, x * HD : (x + 1) * HD].astype(jnp.bfloat16)


def project(member, hidden, w_kv):
    return pl.pallas_call(
        project_kernel,
        out_shape=[struct((4, 4, TOK, HD), jnp.bfloat16), TOKEN],
        in_specs=[SMEM, ANY, ANY],
        out_specs=[VMEM] * 2,
        scratch_shapes=[
            pltpu.VMEM((TOK, FEATURES), jnp.bfloat16),
            pltpu.VMEM((4, FEATURES, 4 * HD), jnp.bfloat16),
            pltpu.SemaphoreType.DMA((5,)),
        ],
        compiler_params=params(12),
        cost_estimate=pl.CostEstimate(
            flops=2 * TOK * FEATURES * 2048, bytes_accessed=4 << 20, transcendentals=0
        ),
        name="project",
    )(member, in_hbm(hidden), in_hbm(w_kv))


def sum_x_kernel(member_ref, parts_ref, after_ref, keep_ref, send_ref, token_ref):
    token_ref[...] = after_ref[...]
    zh = member_ref[0] // 4
    for k in range(4):
        total = parts_ref[0, k].astype(jnp.float32)
        for x in (1, 2, 3):
            total = total + parts_ref[x, k].astype(jnp.float32)
        if k == 0:
            keep_ref[...] = total
        send_ref[zh ^ k] = total.astype(jnp.bfloat16)


def sum_x(member, parts, after):
    return pl.pallas_call(
        sum_x_kernel,
        out_shape=[
            struct((TOK, HD), jnp.float32),
            struct((4, TOK, HD), jnp.bfloat16),
            TOKEN,
        ],
        in_specs=[SMEM] + [VMEM] * 2,
        out_specs=[VMEM] * 3,
        compiler_params=params(10),
        name="sum_x",
    )(member, parts, after)


def finish_kernel(member_ref, keep_ref, parts_ref, cosine_ref, sine_ref, after_ref, out_ref, send_ref):
    zh = member_ref[0] // 4
    total = keep_ref[...]
    for k in (1, 2, 3):
        total = total + parts_ref[zh ^ k].astype(jnp.float32)
    turned = pltpu.roll(total, HD // 2, 1)
    done = (total * cosine_ref[...] + turned * sine_ref[...]).astype(jnp.bfloat16)
    out_ref[...] = done
    for at in range(4):
        send_ref[at] = done


def finish(member, keep, parts, cosine, sine, after):
    return pl.pallas_call(
        finish_kernel,
        out_shape=[struct((TOK, HD), jnp.bfloat16), struct((4, TOK, HD), jnp.bfloat16)],
        in_specs=[SMEM] + [VMEM] * 5,
        out_specs=[VMEM] * 2,
        compiler_params=params(8),
        name="finish",
    )(member, keep, parts, cosine, sine, after)


def source_of(pairing_ref, target):
    source = jnp.int32(0)
    for i in range(16):
        source = jnp.where(pairing_ref[i] == target, i, source)
    return source


def choose(index, refs):
    block = refs[0][...]
    for at in range(1, len(refs)):
        block = jnp.where(index == at, refs[at][...], block)
    return block


def offer_kernel(pairing_ref, inst_ref, *refs):
    column, outs = refs[0], refs[1:]
    inst = inst_ref[0]
    for j in range(4):
        source = source_of(pairing_ref, inst ^ (4 * j))
        outs[j][...] = column[source & 3]


def offer(pairing, inst, column):
    return pl.pallas_call(
        offer_kernel,
        out_shape=[struct((TOK, HD), jnp.bfloat16)] * 4,
        in_specs=[SMEM] * 2 + [VMEM],
        out_specs=[VMEM] * 4,
        compiler_params=params(8),
        name="offer",
    )(pairing, inst, column)


def take_kernel(pairing_ref, inst_ref, role_ref, own_ref, *refs):
    offers, out_ref = refs[:4], refs[5]
    inst = inst_ref[0]
    handed = choose((source_of(pairing_ref, inst) ^ inst) // 4, offers[::-1])
    out_ref[...] = jnp.where(role_ref[0] == 1, handed, own_ref[...])


def take(pairing, inst, role, own_kv, offers, after):
    return pl.pallas_call(
        take_kernel,
        out_shape=struct((TOK, HD), jnp.bfloat16),
        in_specs=[SMEM] * 3 + [VMEM] * 6,
        out_specs=VMEM,
        compiler_params=params(8),
        name="take",
    )(pairing, inst, role, own_kv, *offers, after)


def dot_rows(a, b):
    return lax.dot_general(a, b, (((1,), (1,)), ((), ())), preferred_element_type=jnp.float32)


def load_cache(valid, kv_ref, keys, values):
    inside = lax.broadcasted_iota(jnp.int32, keys.shape, 0) < valid
    rows = kv_ref[0]
    keys[...] = jnp.where(inside, rows, jnp.broadcast_to(rows[:1], rows.shape))
    values[:, :HD] = jnp.where(inside, kv_ref[1], 0)
    values[:, HD:] = jnp.where(inside, 1.0, 0.0).astype(jnp.bfloat16)


def update(top, ext, scores, values):
    peak = jnp.max(scores, axis=1, keepdims=True) * SCALE
    if top is not None:
        peak = jnp.maximum(top, peak)
    weights = jnp.exp2(scores * SCALE - peak).astype(jnp.bfloat16)
    term = jnp.dot(weights, values, preferred_element_type=jnp.float32)
    if top is not None:
        term = ext * jnp.exp2(top - peak) + term
    return peak, term


def over_cache(top, ext, queried, keys, values):
    for at in range(0, keys.shape[0], SUB):
        scores = dot_rows(queried, keys[at : at + SUB, :])
        top, ext = update(top, ext, scores, values[at : at + SUB, :])
    return top, ext


def merge(state, other):
    (top, total, acc), (other_top, other_total, other_acc) = state, other
    peak = jnp.maximum(top, other_top)
    scale, other_scale = jnp.exp2(top - peak), jnp.exp2(other_top - peak)
    return peak, total * scale + other_total * other_scale, acc * scale + other_acc * other_scale


def valid_slots(length_ref, member_ref, own, at, count):
    limit = length_ref[0] * BLOCK
    low = jnp.minimum(limit, HALF)
    first_half = (member_ref[0] % 2 == 0) == own
    return jnp.clip(jnp.where(first_half, low, limit - low) - at, 0, count)


def cache_part_kernel(own, at_slot, length_ref, member_ref, q_ref, kv_ref, after_ref, *refs):
    if own:
        before, (top_ref, total_ref, acc_ref, token_ref, chunk_ref, keys, values) = (), refs

        @pl.when(pl.program_id(0) == 0)
        def pass_on():
            chunk_ref[...] = kv_ref[:, : chunk_ref.shape[1], :]

    else:
        before, (top_ref, total_ref, acc_ref, token_ref, keys, values) = refs[:3], refs[3:]
    valid = valid_slots(length_ref, member_ref, own, at_slot, keys.shape[0])

    @pl.when(pl.program_id(0) == 0)
    def prepare():
        token_ref[...] = after_ref[...]
        load_cache(valid, kv_ref, keys, values)

    @pl.when(valid > 0)
    def some():
        for at in range(STEP_HEADS):
            span = slice(at * HD, (at + 1) * HD)
            top, ext = over_cache(None, None, q_ref[:, span], keys, values)
            state = jnp.broadcast_to(top, (TOK, HD)), ext[:, HD:], ext[:, :HD]
            if before:
                state = merge(state, [ref[:, span] for ref in before])
            top_ref[:, span], total_ref[:, span], acc_ref[:, span] = state

    @pl.when(valid <= 0)
    def none():
        for at, ref in enumerate((top_ref, total_ref, acc_ref)):
            ref[...] = before[at][...] if before else jnp.full(ref.shape, 0.0 if at else LOW)


HEADS_SPEC = pl.BlockSpec((TOK, STEP_HEADS * HD), lambda g: (0, g))
ROWS_SPEC = pl.BlockSpec((TOK, HD), lambda g: (0, 0))
TOKEN_SPEC = pl.BlockSpec((8, HD), lambda g: (0, 0))


def cache_part(length, member, queries, cache, after, own, at, state=()):
    count = cache.shape[1]
    return pl.pallas_call(
        functools.partial(cache_part_kernel, own, at),
        grid=(HEADS // STEP_HEADS,),
        out_shape=[pltpu.HBM((TOK, HEADS * HD), jnp.float32)] * 3
        + [TOKEN]
        + [struct((2, HALF, HD), jnp.bfloat16)] * own,
        in_specs=[
            SMEM, SMEM, HEADS_SPEC, pl.BlockSpec(cache.shape, lambda g: (0, 0, 0)), TOKEN_SPEC,
        ]
        + [HEADS_SPEC] * len(state),
        out_specs=[HEADS_SPEC] * 3
        + [TOKEN_SPEC]
        + [pl.BlockSpec((2, HALF, HD), lambda g: (0, 0, 0))] * own,
        scratch_shapes=[
            pltpu.VMEM((count, HD), jnp.bfloat16),
            pltpu.VMEM((count, 2 * HD), jnp.bfloat16),
        ],
        compiler_params=params(20),
        cost_estimate=pl.CostEstimate(
            flops=8 * TOK * HEADS * count * HD,
            bytes_accessed=2 << 20,
            transcendentals=TOK * HEADS * count,
        ),
        name="own_half" if own else "other_part",
    )(length, member, in_hbm(queries), cache, after, *(in_hbm(part) for part in state))


def last_kernel(member_ref, q_ref, *refs):
    before, (mine_ref, theirs_ref) = refs[:3], refs[3:5]
    out_ref, token_ref, new_keys, new_values = refs[5:]
    is_key = member_ref[0] % 2 == 0

    @pl.when(pl.program_id(0) == 0)
    def prepare():
        token_ref[...] = jnp.zeros_like(token_ref)
        new_keys[...] = jnp.where(is_key, mine_ref[...], theirs_ref[...])
        new_values[:, :HD] = jnp.where(is_key, theirs_ref[...], mine_ref[...])
        new_values[:, HD:] = jnp.ones((TOK, HD), jnp.bfloat16)

    row = lax.broadcasted_iota(jnp.int32, (TOK, TOK), 0)
    column = lax.broadcasted_iota(jnp.int32, (TOK, TOK), 1)
    for at in range(STEP_HEADS):
        span = slice(at * HD, (at + 1) * HD)
        scores = jnp.where(column <= row, dot_rows(q_ref[:, span], new_keys[...]), LOW)
        top, ext = update(None, None, scores, new_values[...])
        state = jnp.broadcast_to(top, (TOK, HD)), ext[:, HD:], ext[:, :HD]
        _, total, acc = merge(state, [ref[:, span] for ref in before])
        out_ref[:, span] = (acc / total).astype(jnp.bfloat16)


def last(member, queries, state, mine, theirs):
    return pl.pallas_call(
        last_kernel,
        grid=(HEADS // STEP_HEADS,),
        out_shape=[struct((TOK, HEADS * HD), jnp.bfloat16), TOKEN],
        in_specs=[SMEM] + [HEADS_SPEC] * 4 + [ROWS_SPEC] * 2,
        out_specs=[HEADS_SPEC, TOKEN_SPEC],
        scratch_shapes=[
            pltpu.VMEM((TOK, HD), jnp.bfloat16),
            pltpu.VMEM((TOK, 2 * HD), jnp.bfloat16),
        ],
        compiler_params=params(16),
        cost_estimate=pl.CostEstimate(
            flops=8 * TOK * HEADS * TOK * HD,
            bytes_accessed=3 << 20,
            transcendentals=TOK * HEADS * TOK,
        ),
        name="last",
    )(member, in_hbm(queries), *(in_hbm(part) for part in state), mine, theirs)


def rotation(length, is_key):
    half = HD // 2
    positions = (length * BLOCK + jnp.arange(TOK)).astype(jnp.float32)
    frequency = jnp.exp(jnp.arange(half).astype(jnp.float32) * (-2.0 * math.log(500000.0) / HD))
    angles = positions[:, None] * frequency[None, :]
    cosine = jnp.where(is_key, jnp.cos(angles), 1.0)
    sine = jnp.where(is_key, jnp.sin(angles), 0.0)
    return jnp.concatenate([cosine, cosine], 1), jnp.concatenate([-sine, sine], 1)


def per_device(hidden, queries, prefix_cache, lengths, pairing, w_kv):
    member = lax.axis_index("tp").astype(jnp.int32)
    inst = lax.axis_index("inst").astype(jnp.int32).reshape(1)
    role = lax.axis_index("role").astype(jnp.int32).reshape(1)
    length = lengths.reshape(1)
    resident = prefix_cache[0, 0, 0]
    queried = queries[0, 0]
    cosine, sine = rotation(lengths[0, 0], member % 2 == 0)
    member = member.reshape(1)

    parts, token = project(member, hidden[0, 0], w_kv)
    with jax.named_scope("sum_x"):
        parts = exchange_tp(parts, X_GROUPS)
    *state, token, chunk = cache_part(length, member, queried, in_hbm(resident), token, True, 0)
    with jax.named_scope("prefix_first"):
        across = swap_tp(chunk, 1)
    keep, parts, token = sum_x(member, parts, token)
    with jax.named_scope("sum_z"):
        parts = exchange_tp(parts, Z_GROUPS)
    *state, token = cache_part(length, member, queried, across, token, False, 0, state)
    own_kv, sends = finish(member, keep, parts, cosine, sine, token)

    with jax.named_scope("handoff_y"):
        column = lax.all_to_all(
            sends, "inst", 0, 0, axis_index_groups=Y_GROUPS, tiled=True
        )
    with jax.named_scope("pair"):
        other_kv = swap_tp(own_kv, 1)
    offers = offer(pairing, inst, column)
    with jax.named_scope("handoff_z"):
        offered = [
            role_inst(offers[j], [(i, 16 + (i ^ (4 * j))) for i in range(16)]) for j in range(4)
        ]
    attended, token = last(member, queried, state, own_kv, other_kv)
    layer_kv = take(pairing, inst, role, own_kv, offered[::-1], token)
    return attended[None, None], layer_kv[None, None]


def solution(mesh):
    in_specs = (
        P("role", "inst", None, "tp"),
        P("role", "inst", None, "tp"),
        P("role", "inst", "tp", None, None, None),
        P("role", "inst"),
        P(),
        P("tp", None),
    )
    out_specs = (P("role", "inst", None, "tp"), P("role", "inst", None, "tp"))
    return jax.shard_map(
        per_device, mesh=mesh, in_specs=in_specs, out_specs=out_specs, check_vma=False
    )
```

```python
import functools
import math

import jax
import jax.numpy as jnp
from jax import lax
from jax.experimental import pallas as pl
from jax.experimental.pallas import tpu as pltpu
from jax.sharding import PartitionSpec as P

BLOCK = 128
HD = 128
TOK = 256
HALF = 2048
HEADS = 8
STEP_HEADS = 4
SUB = 512
FEATURES = 512
LOW = -1e30
X_GROUPS = [[z * 4 + x for x in range(4)] for z in range(4)]
Y_GROUPS = [[zl * 4 + y for y in range(4)] for zl in range(4)]
Z_GROUPS = [[z * 4 + x for z in range(4)] for x in range(4)]
SCALE = HD**-0.5 * math.log2(math.e)

SMEM = pl.BlockSpec(memory_space=pltpu.SMEM)
VMEM = pl.BlockSpec(memory_space=pltpu.VMEM)
HBM = pl.BlockSpec(memory_space=pltpu.HBM)
ANY = pl.BlockSpec(memory_space=pl.ANY)


def params(mib):
    return pltpu.CompilerParams(vmem_limit_bytes=mib * 1024 * 1024)


def struct(shape, dtype):
    return jax.ShapeDtypeStruct(shape, dtype)


TOKEN = struct((8, HD), jnp.float32)


def in_hbm(array):
    return pltpu.with_memory_space_constraint(array, pltpu.HBM)


def swap_tp(array, mask):
    return lax.ppermute(array, "tp", [(i, i ^ mask) for i in range(16)])


def exchange_tp(array, groups):
    return lax.all_to_all(array, "tp", 0, 0, axis_index_groups=groups, tiled=True)


def role_inst(array, pairs):
    return lax.ppermute(array, ("role", "inst"), pairs)


def project_kernel(member_ref, hidden_hbm, w_hbm, send_ref, token_ref, hidden_ref, w_ref, sems):
    zh = member_ref[0] // 4
    width = 4 * HD
    copies = [pltpu.make_async_copy(hidden_hbm, hidden_ref, sems.at[4])]
    for k in range(4):
        column = pl.multiple_of((zh ^ k) * width, width)
        copies.append(
            pltpu.make_async_copy(w_hbm.at[:, pl.ds(column, width)], w_ref.at[k], sems.at[k])
        )
    for copy in copies:
        copy.start()
    copies[0].wait()
    token_ref[...] = jnp.zeros_like(token_ref)
    for k in range(4):
        copies[k + 1].wait()
        part = jnp.dot(hidden_ref[...], w_ref[k], preferred_element_type=jnp.float32)
        for x in range(4):
            send_ref[x, k] = part[:, x * HD : (x + 1) * HD].astype(jnp.bfloat16)


def project(member, hidden, w_kv):
    return pl.pallas_call(
        project_kernel,
        out_shape=[struct((4, 4, TOK, HD), jnp.bfloat16), TOKEN],
        in_specs=[SMEM, ANY, ANY],
        out_specs=[VMEM] * 2,
        scratch_shapes=[
            pltpu.VMEM((TOK, FEATURES), jnp.bfloat16),
            pltpu.VMEM((4, FEATURES, 4 * HD), jnp.bfloat16),
            pltpu.SemaphoreType.DMA((5,)),
        ],
        compiler_params=params(12),
        cost_estimate=pl.CostEstimate(
            flops=2 * TOK * FEATURES * 2048, bytes_accessed=4 << 20, transcendentals=0
        ),
        name="project",
    )(member, in_hbm(hidden), in_hbm(w_kv))


def sum_x_kernel(member_ref, parts_ref, after_ref, keep_ref, send_ref, token_ref):
    token_ref[...] = after_ref[...]
    zh = member_ref[0] // 4
    for k in range(4):
        total = parts_ref[0, k].astype(jnp.float32)
        for x in (1, 2, 3):
            total = total + parts_ref[x, k].astype(jnp.float32)
        if k == 0:
            keep_ref[...] = total
        send_ref[zh ^ k] = total.astype(jnp.bfloat16)


def sum_x(member, parts, after):
    return pl.pallas_call(
        sum_x_kernel,
        out_shape=[
            struct((TOK, HD), jnp.float32),
            struct((4, TOK, HD), jnp.bfloat16),
            TOKEN,
        ],
        in_specs=[SMEM] + [VMEM] * 2,
        out_specs=[VMEM] * 3,
        compiler_params=params(10),
        name="sum_x",
    )(member, parts, after)


def finish_kernel(member_ref, keep_ref, parts_ref, cosine_ref, sine_ref, after_ref, out_ref, send_ref):
    zh = member_ref[0] // 4
    total = keep_ref[...]
    for k in (1, 2, 3):
        total = total + parts_ref[zh ^ k].astype(jnp.float32)
    turned = pltpu.roll(total, HD // 2, 1)
    done = (total * cosine_ref[...] + turned * sine_ref[...]).astype(jnp.bfloat16)
    out_ref[...] = done
    for at in range(4):
        send_ref[at] = done


def finish(member, keep, parts, cosine, sine, after):
    return pl.pallas_call(
        finish_kernel,
        out_shape=[struct((TOK, HD), jnp.bfloat16), struct((4, TOK, HD), jnp.bfloat16)],
        in_specs=[SMEM] + [VMEM] * 5,
        out_specs=[VMEM] * 2,
        compiler_params=params(8),
        name="finish",
    )(member, keep, parts, cosine, sine, after)


def source_of(pairing_ref, target):
    source = jnp.int32(0)
    for i in range(16):
        source = jnp.where(pairing_ref[i] == target, i, source)
    return source


def choose(index, refs):
    block = refs[0][...]
    for at in range(1, len(refs)):
        block = jnp.where(index == at, refs[at][...], block)
    return block


def offer_kernel(pairing_ref, inst_ref, *refs):
    column, outs = refs[0], refs[1:]
    inst = inst_ref[0]
    for j in range(4):
        source = source_of(pairing_ref, inst ^ (4 * j))
        outs[j][...] = column[source & 3]


def offer(pairing, inst, column):
    return pl.pallas_call(
        offer_kernel,
        out_shape=[struct((TOK, HD), jnp.bfloat16)] * 4,
        in_specs=[SMEM] * 2 + [VMEM],
        out_specs=[VMEM] * 4,
        compiler_params=params(8),
        name="offer",
    )(pairing, inst, column)


def take_kernel(pairing_ref, inst_ref, role_ref, own_ref, *refs):
    offers, out_ref = refs[:4], refs[5]
    inst = inst_ref[0]
    handed = choose((source_of(pairing_ref, inst) ^ inst) // 4, offers[::-1])
    out_ref[...] = jnp.where(role_ref[0] == 1, handed, own_ref[...])


def take(pairing, inst, role, own_kv, offers, after):
    return pl.pallas_call(
        take_kernel,
        out_shape=struct((TOK, HD), jnp.bfloat16),
        in_specs=[SMEM] * 3 + [VMEM] * 6,
        out_specs=VMEM,
        compiler_params=params(8),
        name="take",
    )(pairing, inst, role, own_kv, *offers, after)


def dot_rows(a, b):
    return lax.dot_general(a, b, (((1,), (1,)), ((), ())), preferred_element_type=jnp.float32)


def load_cache(valid, kv_ref, keys, values):
    inside = lax.broadcasted_iota(jnp.int32, keys.shape, 0) < valid
    rows = kv_ref[0]
    keys[...] = jnp.where(inside, rows, jnp.broadcast_to(rows[:1], rows.shape))
    values[:, :HD] = jnp.where(inside, kv_ref[1], 0)
    values[:, HD:] = jnp.where(inside, 1.0, 0.0).astype(jnp.bfloat16)


def update(top, ext, scores, values):
    peak = jnp.max(scores, axis=1, keepdims=True) * SCALE
    if top is not None:
        peak = jnp.maximum(top, peak)
    weights = jnp.exp2(scores * SCALE - peak).astype(jnp.bfloat16)
    term = jnp.dot(weights, values, preferred_element_type=jnp.float32)
    if top is not None:
        term = ext * jnp.exp2(top - peak) + term
    return peak, term


def over_cache(top, ext, queried, keys, values):
    for at in range(0, keys.shape[0], SUB):
        scores = dot_rows(queried, keys[at : at + SUB, :])
        top, ext = update(top, ext, scores, values[at : at + SUB, :])
    return top, ext


def merge(state, other):
    (top, total, acc), (other_top, other_total, other_acc) = state, other
    peak = jnp.maximum(top, other_top)
    scale, other_scale = jnp.exp2(top - peak), jnp.exp2(other_top - peak)
    return peak, total * scale + other_total * other_scale, acc * scale + other_acc * other_scale


def valid_slots(length_ref, member_ref, own, at, count):
    limit = length_ref[0] * BLOCK
    low = jnp.minimum(limit, HALF)
    first_half = (member_ref[0] % 2 == 0) == own
    return jnp.clip(jnp.where(first_half, low, limit - low) - at, 0, count)


def cache_part_kernel(own, at_slot, length_ref, member_ref, q_ref, kv_ref, after_ref, *refs):
    if own:
        before, (top_ref, total_ref, acc_ref, token_ref, chunk_ref, keys, values) = (), refs

        @pl.when(pl.program_id(0) == 0)
        def pass_on():
            chunk_ref[...] = kv_ref[:, : chunk_ref.shape[1], :]

    else:
        before, (top_ref, total_ref, acc_ref, token_ref, keys, values) = refs[:3], refs[3:]
    valid = valid_slots(length_ref, member_ref, own, at_slot, keys.shape[0])

    @pl.when(pl.program_id(0) == 0)
    def prepare():
        token_ref[...] = after_ref[...]
        load_cache(valid, kv_ref, keys, values)

    @pl.when(valid > 0)
    def some():
        for at in range(STEP_HEADS):
            span = slice(at * HD, (at + 1) * HD)
            top, ext = over_cache(None, None, q_ref[:, span], keys, values)
            state = jnp.broadcast_to(top, (TOK, HD)), ext[:, HD:], ext[:, :HD]
            if before:
                state = merge(state, [ref[:, span] for ref in before])
            top_ref[:, span], total_ref[:, span], acc_ref[:, span] = state

    @pl.when(valid <= 0)
    def none():
        for at, ref in enumerate((top_ref, total_ref, acc_ref)):
            ref[...] = before[at][...] if before else jnp.full(ref.shape, 0.0 if at else LOW)


HEADS_SPEC = pl.BlockSpec((TOK, STEP_HEADS * HD), lambda g: (0, g))
ROWS_SPEC = pl.BlockSpec((TOK, HD), lambda g: (0, 0))
TOKEN_SPEC = pl.BlockSpec((8, HD), lambda g: (0, 0))


def cache_part(length, member, queries, cache, after, own, at, state=()):
    count = cache.shape[1]
    return pl.pallas_call(
        functools.partial(cache_part_kernel, own, at),
        grid=(HEADS // STEP_HEADS,),
        out_shape=[pltpu.HBM((TOK, HEADS * HD), jnp.float32)] * 3
        + [TOKEN]
        + [struct((2, HALF, HD), jnp.bfloat16)] * own,
        in_specs=[
            SMEM, SMEM, HEADS_SPEC, pl.BlockSpec(cache.shape, lambda g: (0, 0, 0)), TOKEN_SPEC,
        ]
        + [HEADS_SPEC] * len(state),
        out_specs=[HEADS_SPEC] * 3
        + [TOKEN_SPEC]
        + [pl.BlockSpec((2, HALF, HD), lambda g: (0, 0, 0))] * own,
        scratch_shapes=[
            pltpu.VMEM((count, HD), jnp.bfloat16),
            pltpu.VMEM((count, 2 * HD), jnp.bfloat16),
        ],
        compiler_params=params(20),
        cost_estimate=pl.CostEstimate(
            flops=8 * TOK * HEADS * count * HD,
            bytes_accessed=2 << 20,
            transcendentals=TOK * HEADS * count,
        ),
        name="own_half" if own else "other_part",
    )(
        length, member, queries if own else in_hbm(queries), cache, after,
        *(in_hbm(part) for part in state),
    )


def last_kernel(member_ref, q_ref, *refs):
    before, (mine_ref, theirs_ref) = refs[:3], refs[3:5]
    out_ref, token_ref, new_keys, new_values = refs[5:]
    is_key = member_ref[0] % 2 == 0

    @pl.when(pl.program_id(0) == 0)
    def prepare():
        token_ref[...] = jnp.zeros_like(token_ref)
        new_keys[...] = jnp.where(is_key, mine_ref[...], theirs_ref[...])
        new_values[:, :HD] = jnp.where(is_key, theirs_ref[...], mine_ref[...])
        new_values[:, HD:] = jnp.ones((TOK, HD), jnp.bfloat16)

    row = lax.broadcasted_iota(jnp.int32, (TOK, TOK), 0)
    column = lax.broadcasted_iota(jnp.int32, (TOK, TOK), 1)
    for at in range(STEP_HEADS):
        span = slice(at * HD, (at + 1) * HD)
        scores = jnp.where(column <= row, dot_rows(q_ref[:, span], new_keys[...]), LOW)
        top, ext = update(None, None, scores, new_values[...])
        state = jnp.broadcast_to(top, (TOK, HD)), ext[:, HD:], ext[:, :HD]
        _, total, acc = merge(state, [ref[:, span] for ref in before])
        out_ref[:, span] = (acc / total).astype(jnp.bfloat16)


def last(member, queries, state, mine, theirs):
    return pl.pallas_call(
        last_kernel,
        grid=(HEADS // STEP_HEADS,),
        out_shape=[struct((TOK, HEADS * HD), jnp.bfloat16), TOKEN],
        in_specs=[SMEM] + [HEADS_SPEC] * 4 + [ROWS_SPEC] * 2,
        out_specs=[HEADS_SPEC, TOKEN_SPEC],
        scratch_shapes=[
            pltpu.VMEM((TOK, HD), jnp.bfloat16),
            pltpu.VMEM((TOK, 2 * HD), jnp.bfloat16),
        ],
        compiler_params=params(16),
        cost_estimate=pl.CostEstimate(
            flops=8 * TOK * HEADS * TOK * HD,
            bytes_accessed=3 << 20,
            transcendentals=TOK * HEADS * TOK,
        ),
        name="last",
    )(member, in_hbm(queries), *(in_hbm(part) for part in state), mine, theirs)


def rotation(length, is_key):
    half = HD // 2
    positions = (length * BLOCK + jnp.arange(TOK)).astype(jnp.float32)
    frequency = jnp.exp(jnp.arange(half).astype(jnp.float32) * (-2.0 * math.log(500000.0) / HD))
    angles = positions[:, None] * frequency[None, :]
    cosine = jnp.where(is_key, jnp.cos(angles), 1.0)
    sine = jnp.where(is_key, jnp.sin(angles), 0.0)
    return jnp.concatenate([cosine, cosine], 1), jnp.concatenate([-sine, sine], 1)


def per_device(hidden, queries, prefix_cache, lengths, pairing, w_kv):
    member = lax.axis_index("tp").astype(jnp.int32)
    inst = lax.axis_index("inst").astype(jnp.int32).reshape(1)
    role = lax.axis_index("role").astype(jnp.int32).reshape(1)
    length = lengths.reshape(1)
    resident = prefix_cache[0, 0, 0]
    queried = queries[0, 0]
    cosine, sine = rotation(lengths[0, 0], member % 2 == 0)
    member = member.reshape(1)

    parts, token = project(member, hidden[0, 0], w_kv)
    with jax.named_scope("sum_x"):
        parts = exchange_tp(parts, X_GROUPS)
    *state, token, chunk = cache_part(length, member, queried, resident, token, True, 0)
    with jax.named_scope("prefix_first"):
        across = swap_tp(chunk, 1)
    keep, parts, token = sum_x(member, parts, token)
    with jax.named_scope("sum_z"):
        parts = exchange_tp(parts, Z_GROUPS)
    *state, token = cache_part(length, member, queried, across, token, False, 0, state)
    own_kv, sends = finish(member, keep, parts, cosine, sine, token)

    with jax.named_scope("handoff_y"):
        column = lax.all_to_all(
            sends, "inst", 0, 0, axis_index_groups=Y_GROUPS, tiled=True
        )
    with jax.named_scope("pair"):
        other_kv = swap_tp(own_kv, 1)
    offers = offer(pairing, inst, column)
    with jax.named_scope("handoff_z"):
        offered = [
            role_inst(offers[j], [(i, 16 + (i ^ (4 * j))) for i in range(16)]) for j in range(4)
        ]
    attended, token = last(member, queried, state, own_kv, other_kv)
    layer_kv = take(pairing, inst, role, own_kv, offered[::-1], token)
    return attended[None, None], layer_kv[None, None]


def solution(mesh):
    in_specs = (
        P("role", "inst", None, "tp"),
        P("role", "inst", None, "tp"),
        P("role", "inst", "tp", None, None, None),
        P("role", "inst"),
        P(),
        P("tp", None),
    )
    out_specs = (P("role", "inst", None, "tp"), P("role", "inst", None, "tp"))
    return jax.shard_map(
        per_device, mesh=mesh, in_specs=in_specs, out_specs=out_specs, check_vma=False
    )
```
